1024 devices in a mesh: dom: 4 (over x_lo, core), brick: 32 (over y, x_hi), slab: 8 (over z).
Axes of the slice: x: 8 (x_hi: 4, x_lo: 2; x = x_hi * 2 + x_lo), y: 8, z: 8, core: 2. Of those that a mesh axis runs over, the one named last changes fastest.
Arguments:
- heat_level: float32 [16, 512, 2048], P('dom', 'brick', 'slab'), may hold values from -6 to 6
- spread_ratio: float32 [16, 512, 2048], P('dom', 'brick', 'slab'), may hold values from 0.02 to 0.12
- stream_courant: float32 [16, 512, 2048], P('dom', 'brick', 'slab'), may hold values from 0 to 0.25
- interface_voxel: int32 [4, 32, 8, 2048], P('dom', 'brick', 'slab'), may hold values from 0 to 4095
- patch_holder_part: int32 [4, 32, 8, 2048, 1], P('dom', 'brick', 'slab'), may hold values from 0 to 31; in each aligned block of 2048 rows (0 to 2047, 2048 to 4095, ..., all dimensions but the last counted through in order) at most 128 rows name the same one
- patch_holder_voxel: int32 [4, 32, 8, 2048], P('dom', 'brick', 'slab'), may hold values from 0 to 4095
- interface_thermal_link: float32 [4, 32, 8, 2048], P('dom', 'brick', 'slab'), may hold values from 0.05 to 0.5
- interface_tally: int32 [4, 32, 8], P('dom', 'brick', 'slab'), may hold values from 1024 to 2048, as said below
Outputs:
- temperature_out: float32 [16, 512, 2048], P('dom', 'brick', 'slab')
The draws below stay inside these ranges and needn't reach their ends.
Inputs may be any that keep to these rules, and one draw needn't show every extreme that they name: `patch_holder_part`: among the 2048 slots of one device no owner brick is named more than 128 times, and some device names one exactly 128 times. `interface_tally`: at least half of each device's slots are live; some device has all of them live.
All inputs are finite; a program needn't handle non-finite values.
Results may differ from the reference program's by a relative error of at most 0.0003.
Values sent between devices are 32-bit elements; how exact they have to be, the bound alone decides.
A program may use at most 32 MiB of HBM per device.

```python
import math
import jax
import jax.numpy as jnp
import numpy as np

PART_DEPTH_NORM = 4
SPAN_SECOND = 16
SPAN_THIRD = 256
SWEEPS = 4
LINER_SLOTS = 2048
CAP = 128
SPAN_FIRST_FULL = 16
SPAN_SECOND_FULL = 512
SPAN_THIRD_FULL = 2048
N_DOM = 4
N_BRICK = 32
N_SLAB = 8


def draw_interface_tally(key, part):
    drawn = jax.random.randint(key, (N_DOM, N_BRICK, N_SLAB), LINER_SLOTS // 2, LINER_SLOTS + 1)
    drawn = drawn.at[0, 0, 0].set(LINER_SLOTS)
    return drawn.at[0, 0, 1].set(LINER_SLOTS // 2).astype(jnp.int32)


def plant(values, key, low, largest):
    index_at = [jax.random.randint(jax.random.fold_in(key, axis), (), 0, length) for axis, length in enumerate(values.shape)]
    longest = values.shape.index(max(values.shape))
    neighbour = index_at[:longest] + [(index_at[longest] + 1) % values.shape[longest]] + index_at[longest + 1:]
    return values.at[tuple(index_at)].set(low).at[tuple(neighbour)].set(largest)


def block_scale(own_key, shape, cuts, smallest, top_value):
    factor_of, own = 1.0, jax.random.fold_in(own_key, 6)
    for axis_at, parts in cuts:
        steps = jnp.exp(jax.random.uniform(jax.random.fold_in(own, axis_at), (parts,), jnp.float32, smallest / len(cuts), top_value / len(cuts)))
        factor_of = factor_of * jnp.repeat(steps, shape[axis_at] // parts).reshape([-1 if axis == axis_at else 1 for axis in range(len(shape))])
    return factor_of


def routed_block(own_key, own, number, rows, number_of, top, reach, slope):
    sequence = jax.random.permutation(own_key, number_of)
    crowded, usual = shares(number_of, rows * top, reach, slope, True), shares(number_of, rows * top, reach, slope, False)
    places = jnp.arange(number_of)

    def named(tallies, rotation):
        used = int((tallies > 0).sum())
        fixed = max(1, used // 4)
        moved = fixed + (places - fixed + rotation * (used - fixed)) % max(1, number_of - fixed)
        return jnp.zeros((number_of,), jnp.int32).at[sequence[jnp.where(places < fixed, places, moved)]].set(jnp.asarray(tallies, jnp.int32))

    tallies = jnp.where(number % 4 == 0, named(crowded, number // 4), named(usual, number - number // 4 - 1))
    mixed = jax.random.permutation(jax.random.fold_in(own, 3), number_of)
    giver, receiver = mixed[0:number_of // 2 * 2:2], mixed[1:number_of // 2 * 2:2]
    room = jnp.minimum(tallies[giver] - 1, reach - tallies[receiver]) // 2
    room = jnp.where((giver == sequence[0]) | (receiver == sequence[0]) | (tallies[receiver] == 0), 0, jnp.maximum(room, 0))
    moved = jax.random.randint(jax.random.fold_in(own, 4), (number_of // 2,), 0, 1 << 20) % (room + 1)
    tallies = tallies.at[giver].add(-moved).at[receiver].add(moved)
    items = jnp.searchsorted(jnp.cumsum(tallies), jnp.arange(rows * top), side="right").astype(jnp.int32)
    grid = items.reshape(top, rows).T
    grid = grid[jax.random.permutation(jax.random.fold_in(own, 1), rows)]
    rotation = jax.random.randint(jax.random.fold_in(own, 2), (rows, 1), 0, top)
    return jnp.take_along_axis(grid, (jnp.arange(top)[None, :] + rotation) % top, axis=1)


def shares(number_of, total, limit, skew, full):
    loads = [(1 << 20) // math.isqrt(rank ** skew) + 1 for rank in range(1, number_of + 1)]
    largest = limit if full else min(limit, max(-(-total // number_of), total * loads[0] // sum(loads)))
    least = 1 if total - largest >= number_of - 1 else 0
    counts, surplus = [largest] + [least] * (number_of - 1), total - largest - least * (number_of - 1)
    while surplus > 0:
        free = [i for i in range(1, number_of) if counts[i] < largest] or [i for i in range(1, number_of) if counts[i] < limit]
        pool, remaining = sum([loads[i] for i in free]), surplus
        for i in free:
            extra = min(limit - counts[i], max(1, remaining * loads[i] // pool), surplus)
            counts[i] = counts[i] + extra
            surplus = surplus - extra
    return np.array(counts)


def noise(own_key, shape, spread, bound, shards=(), kind=jnp.bfloat16):
    result = jax.random.normal(own_key, shape, jnp.float32) * spread
    if len(shards) > 0:
        result = block_scale(own_key, shape, shards, -0.22, 0.18) * result
    return jnp.clip(result, min=-bound, max=bound).astype(kind)


def setup_inputs(seed: int = 0) -> dict:
    streams_of = jax.random.split(jax.random.key(seed), 9)
    heat_level = noise(streams_of[0], (SPAN_FIRST_FULL, SPAN_SECOND_FULL, SPAN_THIRD_FULL), 1.0, 6.0, ((0, 4), (1, 32), (2, 8)), jnp.float32)
    spread_ratio = jnp.clip(0.02 + 0.09999999776482582 * jax.random.uniform(streams_of[1], (SPAN_FIRST_FULL, SPAN_SECOND_FULL, SPAN_THIRD_FULL), jnp.float32) ** block_scale(streams_of[1], (SPAN_FIRST_FULL, SPAN_SECOND_FULL, SPAN_THIRD_FULL), ((0, 4), (1, 32), (2, 8)), -0.2, 0.2), 0.02, 0.12)
    stream_courant = jnp.clip(0.25 * jax.random.uniform(streams_of[2], (SPAN_FIRST_FULL, SPAN_SECOND_FULL, SPAN_THIRD_FULL), jnp.float32) ** block_scale(streams_of[2], (SPAN_FIRST_FULL, SPAN_SECOND_FULL, SPAN_THIRD_FULL), ((0, 4), (1, 32), (2, 8)), -0.2, 0.2), 0.0, 0.25)
    interface_voxel = plant(jax.random.randint(streams_of[3], (N_DOM, N_BRICK, N_SLAB, LINER_SLOTS), 0, SPAN_SECOND * SPAN_THIRD), jax.random.fold_in(streams_of[3], 1), 0, (SPAN_SECOND * SPAN_THIRD) - 1).astype(jnp.int32)
    patch_holder_part_keys = jax.random.split(jax.random.fold_in(streams_of[4], 1), N_DOM * N_BRICK * N_SLAB * LINER_SLOTS // LINER_SLOTS)
    patch_holder_part_turns = jax.random.permutation(jax.random.fold_in(streams_of[4], 3), N_DOM * N_BRICK * N_SLAB * LINER_SLOTS // LINER_SLOTS)
    patch_holder_part = jax.vmap(lambda own, number: routed_block(jax.random.fold_in(streams_of[4], 2), own, number, LINER_SLOTS, N_BRICK, 1, CAP, 2))(patch_holder_part_keys, patch_holder_part_turns).reshape((N_DOM, N_BRICK, N_SLAB, LINER_SLOTS, 1))
    patch_holder_voxel = plant(jax.random.randint(streams_of[5], (N_DOM, N_BRICK, N_SLAB, LINER_SLOTS), 0, SPAN_SECOND * SPAN_THIRD), jax.random.fold_in(streams_of[5], 1), 0, (SPAN_SECOND * SPAN_THIRD) - 1).astype(jnp.int32)
    interface_thermal_link = jnp.clip(jnp.exp(math.log(0.5) - 2.3025851 * jax.random.uniform(streams_of[6], (N_DOM, N_BRICK, N_SLAB, LINER_SLOTS), jnp.float32) ** block_scale(streams_of[6], (N_DOM, N_BRICK, N_SLAB, LINER_SLOTS), ((0, 4), (1, 32), (2, 8)), -0.2, 0.2)), 0.05, 0.5)
    interface_tally = draw_interface_tally(jax.random.fold_in(streams_of[8], 71), 0)
    return {"heat_level": heat_level, "spread_ratio": spread_ratio, "stream_courant": stream_courant, "interface_voxel": interface_voxel, "patch_holder_part": patch_holder_part, "patch_holder_voxel": patch_holder_voxel, "interface_thermal_link": interface_thermal_link, "interface_tally": interface_tally}


def iterate_every(heat_level_mesh, spread_ratio, advect_speed):
    margin_extended = jnp.pad(heat_level_mesh, ((0, 0), (1, 1), (1, 1), (1, 1)))
    middle_value = heat_level_mesh
    beside = margin_extended[:, 2:, 1:-1, 1:-1] + margin_extended[:, :-2, 1:-1, 1:-1] + margin_extended[:, 1:-1, 2:, 1:-1] + margin_extended[:, 1:-1, :-2, 1:-1] + margin_extended[:, 1:-1, 1:-1, 2:] + margin_extended[:, 1:-1, 1:-1, :-2]
    return middle_value + spread_ratio * (beside - 6.0 * middle_value) - advect_speed * (middle_value - margin_extended[:, 1:-1, 1:-1, :-2])


def sheet_stack(heat_level_mesh):
    leading_sheet = heat_level_mesh[:, 0].reshape(N_DOM, N_BRICK, SPAN_SECOND, N_SLAB, SPAN_THIRD)
    return leading_sheet.transpose(0, 1, 3, 2, 4).reshape(N_DOM * N_BRICK * N_SLAB, SPAN_SECOND * SPAN_THIRD)


def flatten_sheets(flat_rows):
    shaped = flat_rows.reshape(N_DOM, N_BRICK, N_SLAB, SPAN_SECOND, SPAN_THIRD).transpose(0, 1, 3, 2, 4)
    return shaped.reshape(N_DOM, N_BRICK * SPAN_SECOND, N_SLAB * SPAN_THIRD)


def bundle_interfaces(liner_sheet, liner_voxels, owner_brick, land_cell, thermal_link, face_count, solid_flag):
    face_total = liner_voxels.shape[0]
    enabled_mask = (jnp.arange(face_total) < face_count) & (solid_flag < 0.5)
    onehot = ((owner_brick[:, None] == jnp.arange(N_BRICK)[None, :]) & enabled_mask[:, None]).astype(jnp.int32)
    slot_rank = jnp.sum(jnp.cumsum(onehot, axis=0) * onehot, axis=1) - 1
    position_number = jnp.where(enabled_mask, owner_brick * CAP + slot_rank, N_BRICK * CAP).astype(jnp.int32)
    packed_rows = jnp.stack([liner_sheet[liner_voxels], thermal_link, land_cell.astype(jnp.float32)])
    packet = jnp.zeros((3, N_BRICK * CAP + 1), jnp.float32).at[:, position_number].set(packed_rows)[:, :N_BRICK * CAP]
    return packet, position_number, enabled_mask


def collect_sources(packed_rows):
    land_cell = packed_rows[2].astype(jnp.int32)
    solid_conduct = jnp.zeros((SPAN_SECOND * SPAN_THIRD,), jnp.float32).at[land_cell].add(packed_rows[1])
    solid_source = jnp.zeros((SPAN_SECOND * SPAN_THIRD,), jnp.float32).at[land_cell].add(packed_rows[1] * packed_rows[0])
    return solid_conduct, solid_source


def gas_sources(liner_voxels, weight, wall_temp):
    fluid_link = jnp.zeros((SPAN_SECOND * SPAN_THIRD,), jnp.float32).at[liner_voxels].add(weight)
    fluid_input = jnp.zeros((SPAN_SECOND * SPAN_THIRD,), jnp.float32).at[liner_voxels].add(weight * wall_temp)
    return fluid_link, fluid_input


def reference(heat_level, spread_ratio, stream_courant, interface_voxel, patch_holder_part, patch_holder_voxel, interface_thermal_link, interface_tally):
    processor_number = N_DOM * N_BRICK * N_SLAB
    solid_dom = (jnp.arange(N_DOM) == N_DOM - 1).astype(jnp.float32)
    heat_level_mesh = heat_level.reshape(N_DOM, PART_DEPTH_NORM, SPAN_SECOND_FULL, SPAN_THIRD_FULL)
    spread_ratio = spread_ratio.reshape(N_DOM, PART_DEPTH_NORM, SPAN_SECOND_FULL, SPAN_THIRD_FULL)
    advect_speed = stream_courant.reshape(N_DOM, PART_DEPTH_NORM, SPAN_SECOND_FULL, SPAN_THIRD_FULL) * (1.0 - solid_dom)[:, None, None, None]
    marker_partition = jnp.broadcast_to(solid_dom[:, None, None], (N_DOM, N_BRICK, N_SLAB)).reshape(processor_number)
    for repeat in range(SWEEPS):
        heat_level_mesh = iterate_every(heat_level_mesh, spread_ratio, advect_speed)
    liner_voxels = interface_voxel.reshape(processor_number, LINER_SLOTS)
    thermal_link = interface_thermal_link.reshape(processor_number, LINER_SLOTS)
    message_bundles, position_number, enabled_mask = jax.vmap(bundle_interfaces)(sheet_stack(heat_level_mesh), liner_voxels, patch_holder_part.reshape(processor_number, LINER_SLOTS), patch_holder_voxel.reshape(processor_number, LINER_SLOTS), thermal_link, interface_tally.reshape(processor_number), marker_partition)
    arrived = message_bundles.reshape(N_DOM, N_BRICK, N_SLAB, 3, N_BRICK, CAP).transpose(4, 2, 3, 0, 1, 5)
    arrived = arrived.reshape(N_BRICK * N_SLAB, 3, N_DOM * N_BRICK * CAP)
    solid_conduct, solid_source = jax.vmap(collect_sources)(arrived)
    solid_conduct = jnp.broadcast_to(solid_conduct[None], (N_DOM, N_BRICK * N_SLAB, SPAN_SECOND * SPAN_THIRD)).reshape(processor_number, SPAN_SECOND * SPAN_THIRD)
    solid_source = jnp.broadcast_to(solid_source[None], (N_DOM, N_BRICK * N_SLAB, SPAN_SECOND * SPAN_THIRD)).reshape(processor_number, SPAN_SECOND * SPAN_THIRD)
    for repeat in range(SWEEPS):
        liner_previous = sheet_stack(heat_level_mesh)
        heat_level_mesh = iterate_every(heat_level_mesh, spread_ratio, advect_speed)
        summand_piece = marker_partition[:, None] * (solid_source - solid_conduct * liner_previous) / (1.0 + solid_conduct)
        heat_level_mesh = heat_level_mesh.at[:, 0].add(flatten_sheets(summand_piece))
    liner_current = sheet_stack(heat_level_mesh).reshape(N_DOM, N_BRICK * N_SLAB, SPAN_SECOND * SPAN_THIRD)[N_DOM - 1]
    land_cell = arrived[:, 2].astype(jnp.int32)
    answer = jnp.take_along_axis(liner_current, land_cell, axis=1)
    answer = answer.reshape(N_BRICK, N_SLAB, N_DOM, N_BRICK, CAP).transpose(2, 3, 1, 0, 4).reshape(processor_number, N_BRICK * CAP)
    wall_temp = jnp.take_along_axis(answer, jnp.minimum(position_number, N_BRICK * CAP - 1), axis=1)
    weight = jnp.where(enabled_mask, thermal_link, 0.0)
    fluid_link, fluid_input = jax.vmap(gas_sources)(liner_voxels, weight, wall_temp)
    sheet_current = sheet_stack(heat_level_mesh)
    heat_level_mesh = heat_level_mesh.at[:, 0].add(flatten_sheets((fluid_input - fluid_link * sheet_current) / (1.0 + fluid_link)))
    return heat_level_mesh.reshape(SPAN_FIRST_FULL, SPAN_SECOND_FULL, SPAN_THIRD_FULL)
```

```python
import functools
import math

import jax
import jax.numpy as jnp
from jax import lax
from jax.experimental import pallas as pl
from jax.experimental.pallas import tpu as pltpu
from jax.sharding import PartitionSpec as P

SWEEPS = 4
W = 4
CAP = 128
LAYERS, ROWS, COLS = 4, 16, 256
XR, XC = ROWS + 8, COLS + 128
PARTS = 7
STEPS = ((-1, 0), (1, 0), (0, -1), (0, 1), (-1, -1), (-1, 1), (1, -1), (1, 1))
MESH = pl.DeviceIdType.MESH
F32, BF16, I32 = jnp.float32, jnp.bfloat16, jnp.int32
NT = (((1,), (1,)), ((), ()))
NN = (((1,), (0,)), ((), ()))


def iota(shape, dim):
    return lax.broadcasted_iota(I32, shape, dim)


def dot(a, b, dims):
    return lax.dot_general(a, b, dims, preferred_element_type=F32)


def split2(x):
    high = x.astype(BF16).astype(F32)
    return high, x - high


def kernel(
    nd, nb, ns,
    heat, ratio, courant, voxel_h, owner_h, target_h, link_h, tally,
    out,
    ua, ub, rx, cx, gx, sx,
    voxel, owner, target, link,
    ysend, zsend, yst, zst, dst8,
    uy, uz, udg, gy, gz, gdg, sy, sz, sdg,
    hot, owner_hot, prefix, meta_a, meta_b,
    cell_y, cell_z, link_p, q_rows, wall_rows, hsum,
    meta_send, q_send, meta_recv, q_recv, ans_send, wall_recv,
    in_sem, slot_sem, out_sem,
    a_send, a_recv, u_send, u_recv, g_send, g_recv, s_send, s_recv,
    meta_ssem, meta_rsem, q_ssem, q_rsem, ans_ssem, ans_rsem,
):
    dom, brick, slab = lax.axis_index("dom"), lax.axis_index("brick"), lax.axis_index("slab")
    last = nd - 1
    solid = dom == last
    rows_in = last * nb

    own = (slice(None), pl.ds(0, ROWS), pl.ds(0, COLS))
    fields = [
        pltpu.make_async_copy(h, x.at[own], in_sem.at[i])
        for i, (h, x) in enumerate(((heat, ua), (ratio, rx), (courant, cx)))
    ]
    slots = [
        pltpu.make_async_copy(h, v, slot_sem.at[i])
        for i, (h, v) in enumerate(((owner_h, owner), (voxel_h, voxel), (target_h, target), (link_h, link)))
    ]
    for copy in fields:
        copy.start()
    for copy in slots:
        copy.start()

    def neighbour(step):
        db, dz = step
        return (dom, lax.rem(brick + db + nb, nb), lax.rem(slab + dz + ns, ns))

    barrier = pltpu.get_barrier_semaphore()
    for step in STEPS:
        pl.semaphore_signal(barrier, inc=1, device_id=neighbour(step), device_id_type=MESH)

    @pl.when(solid)
    def _():
        def greet(i, _):
            for d in range(last):
                to = lax.rem(brick + i, nb)
                pl.semaphore_signal(barrier, inc=1, device_id=(d, to, slab), device_id_type=MESH)
            return 0

        lax.fori_loop(0, nb, greet, 0)

    @pl.when(jnp.logical_not(solid))
    def _():
        def greet(i, _):
            to = lax.rem(brick + i, nb)
            pl.semaphore_signal(barrier, inc=1, device_id=(last, to, slab), device_id_type=MESH)
            return 0

        lax.fori_loop(0, nb, greet, 0)

    gas = jnp.where(solid, 0.0, 1.0).astype(F32)
    more_b = jnp.where(brick < nb - 1, 1.0, 0.0).astype(F32)
    less_b = jnp.where(brick > 0, 1.0, 0.0).astype(F32)
    more_z = jnp.where(slab < ns - 1, 1.0, 0.0).astype(F32)
    less_z = jnp.where(slab > 0, 1.0, 0.0).astype(F32)

    for copy in fields:
        copy.wait()
    lane16 = iota((ROWS, 128), 1)
    first, final = jnp.zeros((ROWS, 128), F32), jnp.zeros((ROWS, 128), F32)
    packed = jnp.zeros((ROWS, 128), F32)
    for l in range(LAYERS):
        c = cx[l, 0:ROWS, 0:COLS] * gas
        cx[l, 0:ROWS, 0:COLS] = c
        u, r = ua[l, 0:ROWS, 0:COLS], rx[l, 0:ROWS, 0:COLS]
        ysend[0, l] = jnp.concatenate([u[0:W], r[0:W]], axis=0)
        ysend[1, l] = jnp.concatenate([u[ROWS - W:], r[ROWS - W:]], axis=0)
        ysend[0, LAYERS + l // 2, (l % 2) * W:(l % 2) * W + W, :] = c[0:W]
        ysend[1, LAYERS + l // 2, (l % 2) * W:(l % 2) * W + W, :] = c[ROWS - W:]
        for a, x in enumerate((u, r, c)):
            g = (l * 3 + a) * W
            head = pltpu.roll(x[:, 0:128], g, 1) if g else x[:, 0:128]
            tail = pltpu.roll(x[:, 128:256], (64 + g + W) % 128, 1)
            packed = jnp.where((lane16 >= g) & (lane16 < g + W), head, packed)
            packed = jnp.where((lane16 >= 64 + g) & (lane16 < 64 + g + W), tail, packed)
    zsend[...] = packed

    count = jnp.where(solid, len(STEPS) + rows_in, len(STEPS) + nb)
    pl.semaphore_wait(barrier, count)

    def halo_copies(sources, landings, ssem, rsem):
        return [
            pltpu.make_async_remote_copy(
                src_ref=sources[m], dst_ref=landings[m], send_sem=ssem.at[m], recv_sem=rsem.at[m],
                device_id=neighbour(step), device_id_type=MESH,
            )
            for m, step in enumerate(STEPS)
        ]

    low, high = zsend.at[pl.ds(0, 8)], zsend.at[pl.ds(ROWS - 8, 8)]
    a_copies = halo_copies(
        [ysend.at[0], ysend.at[1], zsend, zsend, low, low, high, high],
        [yst.at[0], yst.at[1], zst.at[0], zst.at[1]] + [dst8.at[i] for i in range(4)],
        a_send, a_recv,
    )
    for copy in a_copies:
        copy.start()

    def sheet_copies(x, y, z, d, ssem, rsem):
        def part(r0, rn, c0, cn):
            return x.at[:, pl.ds(r0, rn), pl.ds(c0, cn)]

        return halo_copies(
            [
                part(0, 8, 0, COLS), part(ROWS - 8, 8, 0, COLS),
                part(0, ROWS, 0, 128), part(0, ROWS, COLS - 128, 128),
                part(0, 8, 0, 128), part(0, 8, COLS - 128, 128),
                part(ROWS - 8, 8, 0, 128), part(ROWS - 8, 8, COLS - 128, 128),
            ],
            [y.at[0], y.at[1], z.at[0], z.at[1]] + [d.at[i] for i in range(4)],
            ssem, rsem,
        )

    u_copies = sheet_copies(ua, uy, uz, udg, u_send, u_recv)
    g_copies = sheet_copies(gx, gy, gz, gdg, g_send, g_recv)
    s_copies = sheet_copies(sx, sy, sz, sdg, s_send, s_recv)

    row8 = iota((8, COLS), 0)
    row8n = iota((8, 128), 0)
    lane8 = iota((8, 128), 1)

    def sides(right, left, lanes):
        return jnp.where(lanes < W, right * more_z, jnp.where(lanes >= 128 - W, left * less_z, 0.0))

    def unpack(x, y, z, d, layers):
        for l in range(layers):
            x[l, ROWS:XR, 0:COLS] = jnp.where(row8 < W, y[0, l] * more_b, y[1, l] * less_b)
            x[l, 0:ROWS, COLS:XC] = sides(z[0, l], z[1, l], lane16)
            right = jnp.where(row8n < W, d[0, l] * more_b, d[2, l] * less_b)
            left = jnp.where(row8n < W, d[1, l] * more_b, d[3, l] * less_b)
            x[l, ROWS:XR, COLS:XC] = sides(right, left, lane8)

    @pl.when(jnp.logical_not(solid))
    def _():
        for copy in slots:
            copy.wait()
        live_count = tally[0]
        a, b = iota((128, 128), 0), iota((128, 128), 1)
        before = jnp.concatenate([jnp.where(a < b, 1.0, 0.0), jnp.ones((128, 128), F32)], axis=1).astype(BF16)
        bricks = iota((nb, 128), 0)
        lanes = iota((1, 128), 1)
        groups = owner.shape[0]

        def mark(j, _):
            live = j * 128 + lanes < live_count
            named = jnp.where(live, owner[pl.ds(j, 1), :], nb)
            owner_hot[pl.ds(pl.multiple_of(j * nb, nb), nb), :] = jnp.where(bricks == named, 1.0, 0.0)
            return 0

        lax.fori_loop(0, groups, mark, 0)
        prefix[...] = dot(owner_hot[...].astype(BF16), before, NN)

        def lay(j, carry):
            at = pl.ds(pl.multiple_of(j * nb, nb), nb)
            lane = pl.ds(pl.multiple_of(j * 128, 128), 128)
            one = owner_hot[at, :]
            rank = jnp.sum(one * (prefix[at, 0:128] + carry), axis=0, keepdims=True)
            meta_b[:, lane] = jnp.where(iota((128, 128), 0).astype(F32) == rank, 1.0, 0.0).astype(BF16)
            v, t = voxel[pl.ds(j, 1), :], target[pl.ds(j, 1), :]
            k = link[pl.ds(j, 1), :]
            k1, rest = split2(k)
            k2, k3 = split2(rest)
            values = (
                (v >> 8).astype(F32), (v & 255).astype(F32), (t >> 8).astype(F32), (t & 255).astype(F32),
                k1, k2, k3,
            )
            for q, value in enumerate(values):
                meta_a[q * nb:(q + 1) * nb, lane] = (one * value).astype(BF16)
            return carry + prefix[at, 128:256]

        lax.fori_loop(0, groups, lay, jnp.zeros((nb, 128), F32))
        packet = dot(meta_a[...], meta_b[...], NT)
        part = [packet[q * nb:(q + 1) * nb] for q in range(PARTS)]
        cell_y[...], cell_z[...] = part[0], part[1]
        code = part[2] * 256.0 + part[3]
        k = part[4] + part[5] + part[6]
        link_p[...] = k
        for o in range(nb):
            meta_send[o, 0:1, :] = k[o:o + 1]
            meta_send[o, 1:2, :] = code[o:o + 1]

        def send(i, _):
            to = lax.rem(brick + i, nb)
            pltpu.make_async_remote_copy(
                src_ref=meta_send.at[to], dst_ref=meta_recv.at[dom * nb + brick],
                send_sem=meta_ssem, recv_sem=meta_rsem, device_id=(last, to, slab), device_id_type=MESH,
            ).start()
            return 0

        lax.fori_loop(0, nb, send, 0)

    zrow = iota((COLS, 128), 0).astype(F32)
    yrow = iota((ROWS, 128), 0).astype(F32)

    def hot_columns(z):
        return jnp.where(zrow == z, 1.0, 0.0).astype(BF16)

    def spread(value, y):
        a, b = split2(value)
        there = yrow == y
        return jnp.concatenate([jnp.where(there, a, 0.0), jnp.where(there, b, 0.0)], axis=0).astype(BF16)

    def total(x):
        return x[0:ROWS] + x[ROWS:2 * ROWS]

    def scatter(rows, group, row_of, build):
        def step(g, acc):
            parts, hots = [], []
            for j in range(group):
                value, y, z = row_of(g * group + j)
                parts.append(spread(value, y))
                if build:
                    hots.append(hot_columns(z))
            lane = pl.ds(pl.multiple_of(g * group * 128, 128), group * 128)
            if build:
                columns = jnp.concatenate(hots, axis=1)
                hot[:, lane] = columns
            else:
                columns = hot[:, lane]
            return acc + dot(jnp.concatenate(parts, axis=1), columns, NT)

        return total(lax.fori_loop(0, rows // group, step, jnp.zeros((2 * ROWS, COLS), F32)))

    def sheet_parts(x):
        return jnp.concatenate(split2(x), axis=0).astype(BF16)

    def gather(sheet, g, group, y_of):
        lane = pl.ds(pl.multiple_of(g * group * 128, 128), group * 128)
        got = total(dot(sheet, hot[:, lane], NN))
        return [
            jnp.sum(jnp.where(yrow == y_of(g * group + j), got[:, j * 128:(j + 1) * 128], 0.0), axis=0, keepdims=True)
            for j in range(group)
        ]

    group_p, group_l = math.gcd(8, nb), math.gcd(8, rows_in)

    @pl.when(jnp.logical_not(solid))
    def _():
        def packet_row(i):
            one = pl.ds(i, 1)
            return link_p[one, :], cell_y[one, :], cell_z[one, :]

        hsum[...] = scatter(nb, group_p, packet_row, True)

    for copy in a_copies:
        copy.wait()
    zr = jnp.concatenate([zst[0], jnp.where(row8n < W, dst8[0] * more_b, dst8[2] * less_b)], axis=0)
    zl = jnp.concatenate([zst[1], jnp.where(row8n < W, dst8[1] * more_b, dst8[3] * less_b)], axis=0)
    lane24 = iota((XR, 128), 1)
    for l in range(LAYERS):
        first_u, last_u = yst[0, l], yst[1, l]
        first_c, last_c = yst[0, LAYERS + l // 2], yst[1, LAYERS + l // 2]
        if l % 2:
            first_c = pltpu.roll(first_c, W, 0)
        else:
            last_c = pltpu.roll(last_c, W, 0)
        pairs = (
            (ua, first_u, pltpu.roll(last_u, W, 0)),
            (rx, pltpu.roll(first_u, W, 0), last_u),
            (cx, first_c, last_c),
        )
        for a, (x, after, prior) in enumerate(pairs):
            x[l, ROWS:XR, 0:COLS] = jnp.where(row8 < W, after * more_b, prior * less_b)
            g = (l * 3 + a) * W
            right = pltpu.roll(zr, 128 - g, 1) if g else zr
            left = pltpu.roll(zl, 128 - W - 64 - g, 1)
            x[l, :, COLS:XC] = sides(right, left, lane24)

    def sweep(x, y, source):
        for l in range(LAYERS):
            u = x[l]
            left = pltpu.roll(u, 1, 1)
            around = pltpu.roll(u, 1, 0) + pltpu.roll(u, XR - 1, 0) + left + pltpu.roll(u, XC - 1, 1)
            if l > 0:
                around = around + x[l - 1]
            if l < LAYERS - 1:
                around = around + x[l + 1]
            new = u + rx[l] * (around - 6.0 * u) - cx[l] * (u - left)
            if source and l == 0:
                new = new + (sx[0] - gx[0] * u)
            y[l] = new

    def phase(source):
        for repeat in range(SWEEPS // 2):
            sweep(ua, ub, source)
            sweep(ub, ua, source)

    phase(False)

    @pl.when(jnp.logical_not(solid))
    def _():
        sheet = sheet_parts(ua[0, 0:ROWS, 0:COLS])

        def step(g, _):
            rows = gather(sheet, g, group_p, lambda i: cell_y[pl.ds(i, 1), :])
            for j in range(group_p):
                i = g * group_p + j
                q_send[i] = rows[j] * link_p[pl.ds(i, 1), :]
            return 0

        lax.fori_loop(0, nb // group_p, step, 0)

        def send(i, _):
            to = lax.rem(brick + i, nb)
            pltpu.make_async_remote_copy(
                src_ref=q_send.at[to], dst_ref=q_recv.at[dom * nb + brick],
                send_sem=q_ssem, recv_sem=q_rsem, device_id=(last, to, slab), device_id_type=MESH,
            ).start()
            return 0

        lax.fori_loop(0, nb, send, 0)

    for copy in u_copies:
        copy.start()

    def whole(ref, ssem, rsem):
        return pltpu.make_async_remote_copy(
            src_ref=ref, dst_ref=ref, send_sem=ssem, recv_sem=rsem,
            device_id=neighbour(STEPS[0]), device_id_type=MESH,
        )

    def target_row(i, value):
        code = meta_recv[i, 1:2, :]
        y = jnp.floor(code * (1.0 / 256.0))
        return value, y, code - 256.0 * y

    @pl.when(solid)
    def _():
        for copy in slots:
            copy.wait()
        whole(meta_recv, meta_ssem, meta_rsem).wait_recv()
        gx[0, 0:ROWS, 0:COLS] = scatter(rows_in, group_l, lambda i: target_row(i, meta_recv[i, 0:1, :]), True)
        for copy in g_copies:
            copy.start()

    for copy in u_copies:
        copy.wait()
    unpack(ua, uy, uz, udg, LAYERS)

    @pl.when(solid)
    def _():
        for copy in g_copies:
            copy.wait()
        unpack(gx, gy, gz, gdg, 1)
        g = gx[0]
        inverse = 1.0 / (1.0 + g)
        gx[0] = g * inverse
        whole(q_recv, q_ssem, q_rsem).wait_recv()
        sx[0, 0:ROWS, 0:COLS] = scatter(rows_in, group_l, lambda i: target_row(i, q_recv[i]), False)
        for copy in s_copies:
            copy.start()
        for copy in s_copies:
            copy.wait()
        unpack(sx, sy, sz, sdg, 1)
        sx[0] = sx[0] * inverse
        phase(True)
        sheet = sheet_parts(ua[0, 0:ROWS, 0:COLS])

        def step(g, _):
            rows = gather(sheet, g, group_l, lambda i: target_row(i, None)[1])
            for j in range(group_l):
                i = g * group_l + j
                ans_send[i] = rows[j]
                pltpu.make_async_remote_copy(
                    src_ref=ans_send.at[i], dst_ref=wall_recv.at[brick],
                    send_sem=ans_ssem, recv_sem=ans_rsem,
                    device_id=(lax.div(i, nb), lax.rem(i, nb), slab), device_id_type=MESH,
                ).start()
            return 0

        lax.fori_loop(0, rows_in // group_l, step, 0)
        whole(ans_send, ans_ssem, ans_rsem).wait_send()

    @pl.when(jnp.logical_not(solid))
    def _():
        phase(False)
        whole(meta_send, meta_ssem, meta_rsem).wait_send()
        whole(q_send, q_ssem, q_rsem).wait_send()
        whole(wall_recv, ans_ssem, ans_rsem).wait_recv()

        def packet_row(i):
            one = pl.ds(i, 1)
            return link_p[one, :] * wall_recv[i], cell_y[one, :], None

        q = scatter(nb, group_p, packet_row, False)
        h = hsum[...]
        u = ua[0, 0:ROWS, 0:COLS]
        ua[0, 0:ROWS, 0:COLS] = u + (q - h * u) / (1.0 + h)

    done = pltpu.make_async_copy(ua.at[own], out, out_sem)
    done.start()
    done.wait()


def body(nd, nb, ns, heat, ratio, courant, voxel, owner, target, link, tally):
    groups = voxel.size // 128
    slots = [x.reshape(groups, 128) for x in (voxel, owner, target, link)]
    rows_in = (nd - 1) * nb
    most = max(rows_in, nb)
    vm = pltpu.VMEM
    sem = pltpu.SemaphoreType.DMA

    def stage(layers):
        return [vm((2, layers, 8, COLS), F32), vm((2, layers, ROWS, 128), F32), vm((4, layers, 8, 128), F32)]

    field = vm((LAYERS, XR, XC), F32)
    scratch = (
        [field] * 4 + [vm((1, XR, XC), F32)] * 2
        + [vm((groups, 128), I32)] * 3 + [vm((groups, 128), F32)]
        + [vm((2, LAYERS + 2, 8, COLS), F32), vm((ROWS, 128), F32)]
        + [vm((2, LAYERS + 2, 8, COLS), F32), vm((2, ROWS, 128), F32), vm((4, 8, 128), F32)]
        + stage(LAYERS) + stage(1) + stage(1)
        + [vm((COLS, most * CAP), BF16), vm((groups * nb, 128), F32), vm((groups * nb, 256), F32)]
        + [vm((PARTS * nb, groups * 128), BF16), vm((128, groups * 128), BF16)]
        + [vm((nb, CAP), F32)] * 3 + [vm((nb, CAP), F32)] * 2 + [vm((ROWS, COLS), F32)]
        + [vm((nb, 2, CAP), F32), vm((nb, 1, CAP), F32), vm((rows_in, 2, CAP), F32), vm((rows_in, 1, CAP), F32)]
        + [vm((rows_in, 1, CAP), F32), vm((nb, 1, CAP), F32)]
        + [sem((3,)), sem((4,)), sem]
        + [sem((8,))] * 8
        + [sem] * 6
    )
    hbm = pl.BlockSpec(memory_space=pl.ANY)
    return pl.pallas_call(
        functools.partial(kernel, nd, nb, ns),
        out_shape=jax.ShapeDtypeStruct(heat.shape, F32),
        in_specs=[hbm] * 7 + [pl.BlockSpec(memory_space=pltpu.SMEM)],
        out_specs=hbm,
        scratch_shapes=scratch,
        compiler_params=pltpu.CompilerParams(
            collective_id=0, has_side_effects=True, vmem_limit_bytes=40 * 1024 * 1024
        ),
    )(heat, ratio, courant, *slots, tally.reshape(1))


def solution(mesh):
    nd, nb, ns = (mesh.shape[a] for a in ("dom", "brick", "slab"))
    where = P("dom", "brick", "slab")
    return jax.shard_map(
        functools.partial(body, nd, nb, ns),
        mesh=mesh,
        in_specs=(where,) * 8,
        out_specs=where,
        check_vma=False,
    )
```

```python
import functools
import math

import jax
import jax.numpy as jnp
from jax import lax
from jax.experimental import pallas as pl
from jax.experimental.pallas import tpu as pltpu
from jax.sharding import PartitionSpec as P

SWEEPS = 4
W = 4
CAP = 128
VMEM_BYTES = 60 * 1024 * 1024
LAYERS, ROWS, COLS = 4, 16, 256
XR, XC = ROWS + 8, COLS + 128
PARTS = 7
STEPS = ((-1, 0), (1, 0), (0, -1), (0, 1), (-1, -1), (-1, 1), (1, -1), (1, 1))
MESH = pl.DeviceIdType.MESH
F32, BF16, I32 = jnp.float32, jnp.bfloat16, jnp.int32
NT = (((1,), (1,)), ((), ()))
NN = (((1,), (0,)), ((), ()))


def iota(shape, dim):
    return lax.broadcasted_iota(I32, shape, dim)


def dot(a, b, dims):
    return lax.dot_general(a, b, dims, preferred_element_type=F32)


def split2(x):
    high = x.astype(BF16).astype(F32)
    return high, x - high


def kernel(
    nd, nb, ns,
    heat, ratio, courant, voxel_h, owner_h, target_h, link_h, tally,
    out,
    ua, ub, rx, cx, gx, sx,
    voxel, owner, target, link,
    ysend, zsend, yst, zst, dst8,
    uy, uz, udg, gy, gz, gdg, sy, sz, sdg,
    hot, owner_hot, prefix, meta_a, meta_b,
    cell_y, cell_z, link_p, hsum,
    meta_send, q_send, meta_recv, q_recv, ans_send, wall_recv,
    in_sem, slot_sem, out_sem,
    a_send, a_recv, u_send, u_recv, g_send, g_recv, s_send, s_recv,
    meta_ssem, meta_rsem, q_ssem, q_rsem, ans_ssem, ans_rsem,
):
    dom, brick, slab = lax.axis_index("dom"), lax.axis_index("brick"), lax.axis_index("slab")
    last = nd - 1
    solid = dom == last
    rows_in = last * nb
    wide = math.gcd(4, nb)
    lines = nb // wide
    deep = last * wide
    my_line, my_place = lax.div(brick, wide), lax.rem(brick, wide)
    my_row = my_line * deep + dom * wide + my_place

    def far_first(t):
        k = lax.div(t + 1, 2)
        away = lines // 2 + jnp.where(lax.rem(t, 2) == 0, k, -k)
        return lax.rem(my_line + away + lines, lines)

    own = (slice(None), pl.ds(0, ROWS), pl.ds(0, COLS))
    fields = [
        pltpu.make_async_copy(h, x.at[own], in_sem.at[i])
        for i, (h, x) in enumerate(((heat, ua), (ratio, rx), (courant, cx)))
    ]
    slots = [
        pltpu.make_async_copy(h, v, slot_sem.at[i])
        for i, (h, v) in enumerate(((owner_h, owner), (voxel_h, voxel), (target_h, target), (link_h, link)))
    ]

    def neighbour(step):
        db, dz = step
        return (dom, lax.rem(brick + db + nb, nb), lax.rem(slab + dz + ns, ns))

    def exists(step):
        db, dz = step
        b, z = brick + db, slab + dz
        return (b >= 0) & (b < nb) & (z >= 0) & (z < ns)

    def on(step, act):
        pl.when(exists(step))(act)

    barrier = pltpu.get_barrier_semaphore()
    for step in STEPS:

        @functools.partial(on, step)
        def _():
            pl.semaphore_signal(barrier, inc=1, device_id=neighbour(step), device_id_type=MESH)

    for copy in fields:
        copy.start()
    for copy in slots:
        copy.start()

    @pl.when(solid)
    def _():
        def greet(i, _):
            for d in range(last):
                to = lax.rem(brick + i, nb)
                pl.semaphore_signal(barrier, inc=1, device_id=(d, to, slab), device_id_type=MESH)
            return 0

        lax.fori_loop(0, nb, greet, 0)

    @pl.when(jnp.logical_not(solid))
    def _():
        def greet(i, _):
            to = lax.rem(brick + i, nb)
            pl.semaphore_signal(barrier, inc=1, device_id=(last, to, slab), device_id_type=MESH)
            return 0

        lax.fori_loop(0, nb, greet, 0)

    gas = jnp.where(solid, 0.0, 1.0).astype(F32)
    rows_end = jnp.where(brick < nb - 1, W, 0)
    rows_from = jnp.where(brick > 0, 8 - W, 8)
    lanes_end = jnp.where(slab < ns - 1, W, 0)
    lanes_from = jnp.where(slab > 0, 128 - W, 128)

    for copy in fields:
        copy.wait()
    lane16 = iota((ROWS, 128), 1)
    first, final = jnp.zeros((ROWS, 128), F32), jnp.zeros((ROWS, 128), F32)
    packed = jnp.zeros((ROWS, 128), F32)
    for l in range(LAYERS):
        c = cx[l, 0:ROWS, 0:COLS] * gas
        cx[l, 0:ROWS, 0:COLS] = c
        u, r = ua[l, 0:ROWS, 0:COLS], rx[l, 0:ROWS, 0:COLS]
        ysend[0, l] = jnp.concatenate([u[0:W], r[0:W]], axis=0)
        ysend[1, l] = jnp.concatenate([u[ROWS - W:], r[ROWS - W:]], axis=0)
        ysend[0, LAYERS + l // 2, (l % 2) * W:(l % 2) * W + W, :] = c[0:W]
        ysend[1, LAYERS + l // 2, (l % 2) * W:(l % 2) * W + W, :] = c[ROWS - W:]
        for a, x in enumerate((u, r, c)):
            g = (l * 3 + a) * W
            head = pltpu.roll(x[:, 0:128], g, 1) if g else x[:, 0:128]
            tail = pltpu.roll(x[:, 128:256], (64 + g + W) % 128, 1)
            packed = jnp.where((lane16 >= g) & (lane16 < g + W), head, packed)
            packed = jnp.where((lane16 >= 64 + g) & (lane16 < 64 + g + W), tail, packed)
    zsend[...] = packed

    beside = sum(jnp.where(exists(step), 1, 0) for step in STEPS)
    pl.semaphore_wait(barrier, beside + jnp.where(solid, rows_in, nb))

    def halo_copies(sources, landings, ssem, rsem):
        return [
            pltpu.make_async_remote_copy(
                src_ref=sources[m], dst_ref=landings[m], send_sem=ssem.at[m], recv_sem=rsem.at[m],
                device_id=neighbour(step), device_id_type=MESH,
            )
            for m, step in enumerate(STEPS)
        ]

    def begin(copies):
        for m in reversed(range(len(STEPS))):
            on(STEPS[m], copies[m].start)

    def finish(copies):
        for m, (db, dz) in enumerate(STEPS):
            on((db, dz), copies[m].wait_send)
            on((-db, -dz), copies[m].wait_recv)

    low, high = zsend.at[pl.ds(0, 8)], zsend.at[pl.ds(ROWS - 8, 8)]
    a_copies = halo_copies(
        [ysend.at[0], ysend.at[1], zsend, zsend, low, low, high, high],
        [yst.at[0], yst.at[1], zst.at[0], zst.at[1]] + [dst8.at[i] for i in range(4)],
        a_send, a_recv,
    )
    begin(a_copies)

    def sheet_copies(x, y, z, d, ssem, rsem):
        def part(r0, rn, c0, cn):
            return x.at[:, pl.ds(r0, rn), pl.ds(c0, cn)]

        return halo_copies(
            [
                part(0, 8, 0, COLS), part(ROWS - 8, 8, 0, COLS),
                part(0, ROWS, 0, 128), part(0, ROWS, COLS - 128, 128),
                part(0, 8, 0, 128), part(0, 8, COLS - 128, 128),
                part(ROWS - 8, 8, 0, 128), part(ROWS - 8, 8, COLS - 128, 128),
            ],
            [y.at[0], y.at[1], z.at[0], z.at[1]] + [d.at[i] for i in range(4)],
            ssem, rsem,
        )

    u_copies = sheet_copies(ua, uy, uz, udg, u_send, u_recv)
    g_copies = sheet_copies(gx, gy, gz, gdg, g_send, g_recv)
    s_copies = sheet_copies(sx, sy, sz, sdg, s_send, s_recv)

    row8 = iota((8, COLS), 0)
    row8n = iota((8, 128), 0)
    lane8 = iota((8, 128), 1)

    def sides(right, left, lanes):
        return jnp.where(lanes < lanes_end, right, jnp.where(lanes >= lanes_from, left, 0.0))

    def ends(after, prior, rows):
        return jnp.where(rows < rows_end, after, jnp.where(rows >= rows_from, prior, 0.0))

    def unpack(x, y, z, d, layers):
        for l in range(layers):
            x[l, ROWS:XR, 0:COLS] = ends(y[0, l], y[1, l], row8)
            x[l, 0:ROWS, COLS:XC] = sides(z[0, l], z[1, l], lane16)
            right = ends(d[0, l], d[2, l], row8n)
            left = ends(d[1, l], d[3, l], row8n)
            x[l, ROWS:XR, COLS:XC] = sides(right, left, lane8)

    @pl.when(jnp.logical_not(solid))
    def _():
        for copy in slots:
            copy.wait()
        live_count = tally[0]
        a, b = iota((128, 128), 0), iota((128, 128), 1)
        before = jnp.concatenate([jnp.where(a < b, 1.0, 0.0), jnp.ones((128, 128), F32)], axis=1).astype(BF16)
        bricks = iota((nb, 128), 0)
        lanes = iota((1, 128), 1)
        groups = owner.shape[0]

        def mark(j, _):
            live = j * 128 + lanes < live_count
            named = jnp.where(live, owner[pl.ds(j, 1), :], nb)
            owner_hot[pl.ds(pl.multiple_of(j * nb, nb), nb), :] = jnp.where(bricks == named, 1.0, 0.0)
            return 0

        lax.fori_loop(0, groups, mark, 0)
        prefix[...] = dot(owner_hot[...].astype(BF16), before, NN)

        def lay(j, carry):
            at = pl.ds(pl.multiple_of(j * nb, nb), nb)
            lane = pl.ds(pl.multiple_of(j * 128, 128), 128)
            one = owner_hot[at, :]
            rank = jnp.sum(one * (prefix[at, 0:128] + carry), axis=0, keepdims=True)
            meta_b[:, lane] = jnp.where(iota((128, 128), 0).astype(F32) == rank, 1.0, 0.0).astype(BF16)
            v, t = voxel[pl.ds(j, 1), :], target[pl.ds(j, 1), :]
            k = link[pl.ds(j, 1), :]
            k1, rest = split2(k)
            k2, k3 = split2(rest)
            values = (
                (v >> 8).astype(F32), (v & 255).astype(F32), (t >> 8).astype(F32), (t & 255).astype(F32),
                k1, k2, k3,
            )
            for q, value in enumerate(values):
                meta_a[q * nb:(q + 1) * nb, lane] = (one * value).astype(BF16)
            return carry + prefix[at, 128:256]

        lax.fori_loop(0, groups, lay, jnp.zeros((nb, 128), F32))
        packet = dot(meta_a[...], meta_b[...], NT)
        part = [packet[q * nb:(q + 1) * nb] for q in range(PARTS)]
        cell_y[...], cell_z[...] = part[0], part[1]
        code = part[2] * 256.0 + part[3]
        k = part[4] + part[5] + part[6]
        link_p[...] = k
        for o in range(nb):
            meta_send[o, 0:1, :] = k[o:o + 1]
            meta_send[o, 1:2, :] = code[o:o + 1]

        def send(i, _):
            to = far_first(lax.div(i, wide)) * wide + lax.rem(i, wide)
            pltpu.make_async_remote_copy(
                src_ref=meta_send.at[to], dst_ref=meta_recv.at[my_row],
                send_sem=meta_ssem, recv_sem=meta_rsem.at[my_line], device_id=(last, to, slab), device_id_type=MESH,
            ).start()
            return 0

        lax.fori_loop(0, nb, send, 0)

    zrow = iota((COLS, 128), 0).astype(F32)
    yrow = iota((ROWS, 128), 0).astype(F32)

    def hot_columns(z):
        return jnp.where(zrow == z, 1.0, 0.0).astype(BF16)

    def spread(value, y):
        a, b = split2(value)
        there = yrow == y
        return jnp.concatenate([jnp.where(there, a, 0.0), jnp.where(there, b, 0.0)], axis=0).astype(BF16)

    def total(x):
        return x[0:ROWS] + x[ROWS:2 * ROWS]

    def scatter(steps, group, blocks_of, row_of, build):
        def step(t, acc):
            blocks = blocks_of(t)
            for first in blocks:
                parts, hots = [], []
                for j in range(group):
                    value, y, z = row_of(first + j)
                    parts.append(spread(value, y))
                    if build:
                        hots.append(hot_columns(z))
                lane = pl.ds(pl.multiple_of(first * 128, 128), group * 128)
                if build:
                    columns = jnp.concatenate(hots, axis=1)
                    hot[:, lane] = columns
                else:
                    columns = hot[:, lane]
                acc = acc + dot(jnp.concatenate(parts, axis=1), columns, NT)
            return acc

        return total(lax.fori_loop(0, steps, step, jnp.zeros((2 * ROWS, COLS), F32)))

    def sheet_parts(x):
        return jnp.concatenate(split2(x), axis=0).astype(BF16)

    def gather(sheet, first, group, y_of, put):
        lane = pl.ds(pl.multiple_of(first * 128, 128), group * 128)
        got = total(dot(sheet, hot[:, lane], NN))
        for j in range(group):
            here = jnp.where(yrow == y_of(first + j), got[:, j * 128:(j + 1) * 128], 0.0)
            put(first + j, jnp.sum(here, axis=0, keepdims=True))

    pair = math.gcd(2, lines)
    group_p = math.gcd(8, nb)

    @pl.when(jnp.logical_not(solid))
    def _():
        def packet_row(i):
            one = pl.ds(i, 1)
            return link_p[one, :], cell_y[one, :], cell_z[one, :]

        hsum[...] = scatter(nb // group_p, group_p, lambda t: [t * group_p], packet_row, True)

    finish(a_copies)
    zr = jnp.concatenate([zst[0], ends(dst8[0], dst8[2], row8n)], axis=0)
    zl = jnp.concatenate([zst[1], ends(dst8[1], dst8[3], row8n)], axis=0)
    lane24 = iota((XR, 128), 1)
    for l in range(LAYERS):
        first_u, last_u = yst[0, l], yst[1, l]
        first_c, last_c = yst[0, LAYERS + l // 2], yst[1, LAYERS + l // 2]
        if l % 2:
            first_c = pltpu.roll(first_c, W, 0)
        else:
            last_c = pltpu.roll(last_c, W, 0)
        pairs = (
            (ua, first_u, pltpu.roll(last_u, W, 0)),
            (rx, pltpu.roll(first_u, W, 0), last_u),
            (cx, first_c, last_c),
        )
        for a, (x, after, prior) in enumerate(pairs):
            x[l, ROWS:XR, 0:COLS] = ends(after, prior, row8)
            g = (l * 3 + a) * W
            right = pltpu.roll(zr, 128 - g, 1) if g else zr
            left = pltpu.roll(zl, 128 - W - 64 - g, 1)
            x[l, :, COLS:XC] = sides(right, left, lane24)

    def sweep(x, y, source):
        for l in range(LAYERS):
            u = x[l]
            left = pltpu.roll(u, 1, 1)
            around = pltpu.roll(u, 1, 0) + pltpu.roll(u, XR - 1, 0) + left + pltpu.roll(u, XC - 1, 1)
            if l > 0:
                around = around + x[l - 1]
            if l < LAYERS - 1:
                around = around + x[l + 1]
            new = u + rx[l] * (around - 6.0 * u) - cx[l] * (u - left)
            if source and l == 0:
                new = new + (sx[0] - gx[0] * u)
            y[l] = new

    def phase(source):
        for repeat in range(SWEEPS // 2):
            sweep(ua, ub, source)
            sweep(ub, ua, source)

    phase(False)

    @pl.when(jnp.logical_not(solid))
    def _():
        sheet = sheet_parts(ua[0, 0:ROWS, 0:COLS])

        def put(i, row):
            q_send[i] = row * link_p[pl.ds(i, 1), :]

        def step(t, _):
            firsts = [far_first(t * pair + a) * wide for a in range(pair)]
            for first in firsts:
                gather(sheet, first, wide, lambda i: cell_y[pl.ds(i, 1), :], put)
            for first in firsts:
                for j in range(wide):
                    pltpu.make_async_remote_copy(
                        src_ref=q_send.at[first + j], dst_ref=q_recv.at[my_row],
                        send_sem=q_ssem, recv_sem=q_rsem.at[my_line],
                        device_id=(last, first + j, slab), device_id_type=MESH,
                    ).start()
            return 0

        lax.fori_loop(0, lines // pair, step, 0)

    begin(u_copies)

    def whole(ref, ssem, rsem):
        return pltpu.make_async_remote_copy(
            src_ref=ref, dst_ref=ref, send_sem=ssem, recv_sem=rsem,
            device_id=neighbour(STEPS[0]), device_id_type=MESH,
        )

    def line_in(t, ref, ssem, rsem):
        line = lines - 1 - t
        whole(ref.at[pl.ds(line * deep, deep)], ssem, rsem.at[line]).wait_recv()
        return [line * deep]

    def target_row(i, value):
        code = meta_recv[i, 1:2, :]
        y = jnp.floor(code * (1.0 / 256.0))
        return value, y, code - 256.0 * y

    @pl.when(solid)
    def _():
        for copy in slots:
            copy.wait()
        gx[0, 0:ROWS, 0:COLS] = scatter(
            lines, deep, lambda t: line_in(t, meta_recv, meta_ssem, meta_rsem),
            lambda i: target_row(i, meta_recv[i, 0:1, :]), True,
        )
        begin(g_copies)

    finish(u_copies)
    unpack(ua, uy, uz, udg, LAYERS)

    @pl.when(solid)
    def _():
        finish(g_copies)
        unpack(gx, gy, gz, gdg, 1)
        g = gx[0]
        inverse = 1.0 / (1.0 + g)
        gx[0] = g * inverse
        sx[0, 0:ROWS, 0:COLS] = scatter(
            lines, deep, lambda t: line_in(t, q_recv, q_ssem, q_rsem), lambda i: target_row(i, q_recv[i]), False
        )
        begin(s_copies)
        finish(s_copies)
        unpack(sx, sy, sz, sdg, 1)
        sx[0] = sx[0] * inverse
        phase(True)
        sheet = sheet_parts(ua[0, 0:ROWS, 0:COLS])

        def put(i, row):
            ans_send[i] = row

        def step(t, _):
            to_lines = [far_first(t * pair + a) for a in range(pair)]
            for line in to_lines:
                gather(sheet, line * deep, deep, lambda i: target_row(i, None)[1], put)
            for line in to_lines:
                for j in range(deep):
                    pltpu.make_async_remote_copy(
                        src_ref=ans_send.at[line * deep + j], dst_ref=wall_recv.at[brick],
                        send_sem=ans_ssem, recv_sem=ans_rsem.at[my_line],
                        device_id=(j // wide, line * wide + j % wide, slab), device_id_type=MESH,
                    ).start()
            return 0

        lax.fori_loop(0, lines // pair, step, 0)
        whole(ans_send, ans_ssem, ans_rsem.at[0]).wait_send()

    @pl.when(jnp.logical_not(solid))
    def _():
        phase(False)
        whole(meta_send, meta_ssem, meta_rsem.at[0]).wait_send()
        whole(q_send, q_ssem, q_rsem.at[0]).wait_send()

        def packet_row(i):
            one = pl.ds(i, 1)
            return link_p[one, :] * wall_recv[i], cell_y[one, :], None

        def lines_in(t):
            firsts = []
            for a in range(pair):
                line = far_first(lines - 1 - t * pair - a)
                ref = wall_recv.at[pl.ds(line * wide, wide)]
                whole(ref, ans_ssem, ans_rsem.at[line]).wait_recv()
                firsts.append(line * wide)
            return firsts

        q = scatter(lines // pair, wide, lines_in, packet_row, False)
        h = hsum[...]
        u = ua[0, 0:ROWS, 0:COLS]
        ua[0, 0:ROWS, 0:COLS] = u + (q - h * u) / (1.0 + h)

    done = pltpu.make_async_copy(ua.at[own], out, out_sem)
    done.start()
    done.wait()


def body(nd, nb, ns, heat, ratio, courant, voxel, owner, target, link, tally):
    groups = voxel.size // 128
    slots = [x.reshape(groups, 128) for x in (voxel, owner, target, link)]
    rows_in = (nd - 1) * nb
    most = max(rows_in, nb)
    lines = nb // math.gcd(4, nb)
    vm = pltpu.VMEM
    sem = pltpu.SemaphoreType.DMA

    def stage(layers):
        return [vm((2, layers, 8, COLS), F32), vm((2, layers, ROWS, 128), F32), vm((4, layers, 8, 128), F32)]

    field = vm((LAYERS, XR, XC), F32)
    scratch = (
        [field] * 4 + [vm((1, XR, XC), F32)] * 2
        + [vm((groups, 128), I32)] * 3 + [vm((groups, 128), F32)]
        + [vm((2, LAYERS + 2, 8, COLS), F32), vm((ROWS, 128), F32)]
        + [vm((2, LAYERS + 2, 8, COLS), F32), vm((2, ROWS, 128), F32), vm((4, 8, 128), F32)]
        + stage(LAYERS) + stage(1) + stage(1)
        + [vm((COLS, most * CAP), BF16), vm((groups * nb, 128), F32), vm((groups * nb, 256), F32)]
        + [vm((PARTS * nb, groups * 128), BF16), vm((128, groups * 128), BF16)]
        + [vm((nb, CAP), F32)] * 3 + [vm((ROWS, COLS), F32)]
        + [vm((nb, 2, CAP), F32), vm((nb, 1, CAP), F32), vm((rows_in, 2, CAP), F32), vm((rows_in, 1, CAP), F32)]
        + [vm((rows_in, 1, CAP), F32), vm((nb, 1, CAP), F32)]
        + [sem((3,)), sem((4,)), sem]
        + [sem((8,))] * 8
        + [sem, sem((lines,))] * 3
    )
    hbm = pl.BlockSpec(memory_space=pl.ANY)
    return pl.pallas_call(
        functools.partial(kernel, nd, nb, ns),
        out_shape=jax.ShapeDtypeStruct(heat.shape, F32),
        in_specs=[hbm] * 7 + [pl.BlockSpec(memory_space=pltpu.SMEM)],
        out_specs=hbm,
        scratch_shapes=scratch,
        compiler_params=pltpu.CompilerParams(
            collective_id=0, has_side_effects=True, vmem_limit_bytes=VMEM_BYTES
        ),
    )(heat, ratio, courant, *slots, tally.reshape(1))


def solution(mesh):
    nd, nb, ns = (mesh.shape[a] for a in ("dom", "brick", "slab"))
    where = P("dom", "brick", "slab")
    return jax.shard_map(
        functools.partial(body, nd, nb, ns),
        mesh=mesh,
        in_specs=(where,) * 8,
        out_specs=where,
        check_vma=False,
    )
```

```python
import functools
import math

import jax
import jax.numpy as jnp
from jax import lax
from jax.experimental import pallas as pl
from jax.experimental.pallas import tpu as pltpu
from jax.sharding import PartitionSpec as P

SWEEPS = 4
W = 4
CAP = 128
VMEM_BYTES = 60 * 1024 * 1024
LAYERS, ROWS, COLS = 4, 16, 256
XR, XC = ROWS + 8, COLS + 128
PARTS = 7
STEPS = ((-1, 0), (1, 0), (0, -1), (0, 1), (-1, -1), (-1, 1), (1, -1), (1, 1))
MESH = pl.DeviceIdType.MESH
F32, BF16, I32 = jnp.float32, jnp.bfloat16, jnp.int32
NT = (((1,), (1,)), ((), ()))
NN = (((1,), (0,)), ((), ()))


def iota(shape, dim):
    return lax.broadcasted_iota(I32, shape, dim)


def dot(a, b, dims):
    return lax.dot_general(a, b, dims, preferred_element_type=F32)


def split2(x):
    high = x.astype(BF16).astype(F32)
    return high, x - high


def kernel(
    nd, nb, ns,
    heat, ratio, courant, voxel_h, owner_h, target_h, link_h, tally_h,
    out,
    ua, ub, rx, cx, gx, sx,
    voxel, owner, target, link, tally,
    ysend, zsend, yst, zst, dst8,
    uy, uz, udg, gy, gz, gdg, sy, sz, sdg,
    hot, owner_hot, prefix, meta_a, meta_b,
    cell_y, cell_z, link_p, hsum,
    meta_send, q_send, meta_recv, q_recv, ans_send, wall_recv,
    in_sem, slot_sem, out_sem,
    a_send, a_recv, u_send, u_recv, g_send, g_recv, s_send, s_recv,
    ready, meta_ssem, meta_rsem, q_ssem, q_rsem, ans_ssem, ans_rsem,
):
    dom, brick, slab = lax.axis_index("dom"), lax.axis_index("brick"), lax.axis_index("slab")
    last = nd - 1
    solid = dom == last
    rows_in = last * nb
    wide = math.gcd(4, nb)
    lines = nb // wide
    deep = last * wide
    my_line, my_place = lax.div(brick, wide), lax.rem(brick, wide)
    my_row = my_line * deep + dom * wide + my_place

    def far_first(t):
        k = lax.div(t + 1, 2)
        away = lines // 2 + jnp.where(lax.rem(t, 2) == 0, k, -k)
        return lax.rem(my_line + away + lines, lines)

    own = (slice(None), pl.ds(0, ROWS), pl.ds(0, COLS))
    fields = [
        pltpu.make_async_copy(h, x.at[own], in_sem.at[i])
        for i, (h, x) in enumerate(((heat, ua), (ratio, rx), (courant, cx)))
    ]
    slots = [
        pltpu.make_async_copy(h, v, slot_sem.at[i])
        for i, (h, v) in enumerate(((owner_h, owner), (voxel_h, voxel), (target_h, target), (link_h, link), (tally_h, tally)))
    ]

    def neighbour(step):
        db, dz = step
        return (dom, lax.rem(brick + db + nb, nb), lax.rem(slab + dz + ns, ns))

    def exists(step):
        db, dz = step
        b, z = brick + db, slab + dz
        return (b >= 0) & (b < nb) & (z >= 0) & (z < ns)

    def on(step, act):
        pl.when(exists(step))(act)

    barrier = pltpu.get_barrier_semaphore()

    def greet(*device):
        pl.semaphore_signal(barrier, inc=1, device_id=device, device_id_type=MESH)

    for step in STEPS:
        if step[1] >= 0:

            @functools.partial(on, step)
            def _():
                greet(*neighbour(step))

    @pl.when(solid)
    def _():
        def other(i, _):
            greet(last, lax.rem(my_line + i, lines) * wide + my_place, slab)
            return 0

        lax.fori_loop(1, lines, other, 0)

    @pl.when(jnp.logical_not(solid))
    def _():
        for j in range(wide):
            greet(last, my_line * wide + j, slab)

    for copy in fields:
        copy.start()
    for copy in slots:
        copy.start()

    gas = jnp.where(solid, 0.0, 1.0).astype(F32)
    rows_end = jnp.where(brick < nb - 1, W, 0)
    rows_from = jnp.where(brick > 0, 8 - W, 8)
    lanes_end = jnp.where(slab < ns - 1, W, 0)
    lanes_from = jnp.where(slab > 0, 128 - W, 128)

    for copy in fields:
        copy.wait()
    lane16 = iota((ROWS, 128), 1)
    first, final = jnp.zeros((ROWS, 128), F32), jnp.zeros((ROWS, 128), F32)
    packed = jnp.zeros((ROWS, 128), F32)
    for l in range(LAYERS):
        c = cx[l, 0:ROWS, 0:COLS] * gas
        cx[l, 0:ROWS, 0:COLS] = c
        u, r = ua[l, 0:ROWS, 0:COLS], rx[l, 0:ROWS, 0:COLS]
        ysend[0, l] = jnp.concatenate([u[0:W], r[0:W]], axis=0)
        ysend[1, l] = jnp.concatenate([u[ROWS - W:], r[ROWS - W:]], axis=0)
        ysend[0, LAYERS + l // 2, (l % 2) * W:(l % 2) * W + W, :] = c[0:W]
        ysend[1, LAYERS + l // 2, (l % 2) * W:(l % 2) * W + W, :] = c[ROWS - W:]
        for a, x in enumerate((u, r, c)):
            g = (l * 3 + a) * W
            head = pltpu.roll(x[:, 0:128], g, 1) if g else x[:, 0:128]
            tail = pltpu.roll(x[:, 128:256], (64 + g + W) % 128, 1)
            packed = jnp.where((lane16 >= g) & (lane16 < g + W), head, packed)
            packed = jnp.where((lane16 >= 64 + g) & (lane16 < 64 + g + W), tail, packed)
    zsend[...] = packed

    beside = sum(jnp.where(exists(step), 1, 0) for step in STEPS if step[1] <= 0)
    pl.semaphore_wait(barrier, beside + jnp.where(solid, deep + lines - 1, 0))

    @pl.when(solid)
    def _():
        for d in range(last):
            for j in range(wide):
                pl.semaphore_signal(ready, inc=1, device_id=(d, my_line * wide + j, slab), device_id_type=MESH)

    def halo_copies(sources, landings, ssem, rsem):
        return [
            pltpu.make_async_remote_copy(
                src_ref=sources[m], dst_ref=landings[m], send_sem=ssem.at[m], recv_sem=rsem.at[m],
                device_id=neighbour(step), device_id_type=MESH,
            )
            for m, step in enumerate(STEPS)
        ]

    everywhere = (-1, 0, 1)

    def begin(copies, ways=everywhere):
        for m in reversed(range(len(STEPS))):
            if STEPS[m][1] in ways:
                on(STEPS[m], copies[m].start)

    def arrive(copies, ways):
        for m, (db, dz) in enumerate(STEPS):
            if dz in ways:
                on((-db, -dz), copies[m].wait_recv)

    def leave(copies):
        for step, copy in zip(STEPS, copies):
            on(step, copy.wait_send)

    def finish(copies):
        arrive(copies, everywhere)
        leave(copies)

    low, high = zsend.at[pl.ds(0, 8)], zsend.at[pl.ds(ROWS - 8, 8)]
    a_copies = halo_copies(
        [ysend.at[0], ysend.at[1], zsend, zsend, low, low, high, high],
        [yst.at[0], yst.at[1], zst.at[0], zst.at[1]] + [dst8.at[i] for i in range(4)],
        a_send, a_recv,
    )
    begin(a_copies, (-1, 0))

    def sheet_copies(x, y, z, d, ssem, rsem):
        def part(r0, rn, c0, cn):
            return x.at[:, pl.ds(r0, rn), pl.ds(c0, cn)]

        return halo_copies(
            [
                part(0, 8, 0, COLS), part(ROWS - 8, 8, 0, COLS),
                part(0, ROWS, 0, 128), part(0, ROWS, COLS - 128, 128),
                part(0, 8, 0, 128), part(0, 8, COLS - 128, 128),
                part(ROWS - 8, 8, 0, 128), part(ROWS - 8, 8, COLS - 128, 128),
            ],
            [y.at[0], y.at[1], z.at[0], z.at[1]] + [d.at[i] for i in range(4)],
            ssem, rsem,
        )

    u_copies = sheet_copies(ua, uy, uz, udg, u_send, u_recv)
    g_copies = sheet_copies(gx, gy, gz, gdg, g_send, g_recv)
    s_copies = sheet_copies(sx, sy, sz, sdg, s_send, s_recv)

    row8 = iota((8, COLS), 0)
    row8n = iota((8, 128), 0)
    lane8 = iota((8, 128), 1)

    def sides(right, left, lanes):
        return jnp.where(lanes < lanes_end, right, jnp.where(lanes >= lanes_from, left, 0.0))

    def ends(after, prior, rows):
        return jnp.where(rows < rows_end, after, jnp.where(rows >= rows_from, prior, 0.0))

    def unpack(x, y, z, d, layers):
        for l in range(layers):
            x[l, ROWS:XR, 0:COLS] = ends(y[0, l], y[1, l], row8)
            x[l, 0:ROWS, COLS:XC] = sides(z[0, l], z[1, l], lane16)
            right = ends(d[0, l], d[2, l], row8n)
            left = ends(d[1, l], d[3, l], row8n)
            x[l, ROWS:XR, COLS:XC] = sides(right, left, lane8)

    @pl.when(jnp.logical_not(solid))
    def _():
        for copy in slots:
            copy.wait()
        live_count = tally[0]
        a, b = iota((128, 128), 0), iota((128, 128), 1)
        before = jnp.concatenate([jnp.where(a < b, 1.0, 0.0), jnp.ones((128, 128), F32)], axis=1).astype(BF16)
        bricks = iota((nb, 128), 0)
        lanes = iota((1, 128), 1)
        groups = owner.shape[0]

        def mark(j, _):
            live = j * 128 + lanes < live_count
            named = jnp.where(live, owner[pl.ds(j, 1), :], nb)
            owner_hot[pl.ds(pl.multiple_of(j * nb, nb), nb), :] = jnp.where(bricks == named, 1.0, 0.0)
            return 0

        lax.fori_loop(0, groups, mark, 0)
        prefix[...] = dot(owner_hot[...].astype(BF16), before, NN)

        def lay(j, carry):
            at = pl.ds(pl.multiple_of(j * nb, nb), nb)
            lane = pl.ds(pl.multiple_of(j * 128, 128), 128)
            one = owner_hot[at, :]
            rank = jnp.sum(one * (prefix[at, 0:128] + carry), axis=0, keepdims=True)
            meta_b[:, lane] = jnp.where(iota((128, 128), 0).astype(F32) == rank, 1.0, 0.0).astype(BF16)
            v, t = voxel[pl.ds(j, 1), :], target[pl.ds(j, 1), :]
            k = link[pl.ds(j, 1), :]
            k1, rest = split2(k)
            k2, k3 = split2(rest)
            values = (
                (v >> 8).astype(F32), (v & 255).astype(F32), (t >> 8).astype(F32), (t & 255).astype(F32),
                k1, k2, k3,
            )
            for q, value in enumerate(values):
                meta_a[q * nb:(q + 1) * nb, lane] = (one * value).astype(BF16)
            return carry + prefix[at, 128:256]

        lax.fori_loop(0, groups, lay, jnp.zeros((nb, 128), F32))
        packet = dot(meta_a[...], meta_b[...], NT)
        part = [packet[q * nb:(q + 1) * nb] for q in range(PARTS)]
        cell_y[...], cell_z[...] = part[0], part[1]
        code = part[2] * 256.0 + part[3]
        k = part[4] + part[5] + part[6]
        link_p[...] = k
        for o in range(nb):
            meta_send[o, 0:1, :] = k[o:o + 1]
            meta_send[o, 1:2, :] = code[o:o + 1]

    arrive(a_copies, (-1,))
    begin(a_copies, (1,))

    @pl.when(jnp.logical_not(solid))
    def _():
        pl.semaphore_wait(ready, wide)

        def send(i, _):
            to = far_first(lax.div(i, wide)) * wide + lax.rem(i, wide)
            pltpu.make_async_remote_copy(
                src_ref=meta_send.at[to], dst_ref=meta_recv.at[my_row],
                send_sem=meta_ssem, recv_sem=meta_rsem.at[my_line], device_id=(last, to, slab), device_id_type=MESH,
            ).start()
            return 0

        lax.fori_loop(0, nb, send, 0)

    zrow = iota((COLS, 128), 0).astype(F32)
    yrow = iota((ROWS, 128), 0).astype(F32)

    def hot_columns(z):
        return jnp.where(zrow == z, 1.0, 0.0).astype(BF16)

    def spread(value, y):
        a, b = split2(value)
        there = yrow == y
        return jnp.concatenate([jnp.where(there, a, 0.0), jnp.where(there, b, 0.0)], axis=0).astype(BF16)

    def total(x):
        return x[0:ROWS] + x[ROWS:2 * ROWS]

    def scatter(steps, group, blocks_of, row_of, build):
        def step(t, acc):
            blocks = blocks_of(t)
            for first in blocks:
                parts, hots = [], []
                for j in range(group):
                    value, y, z = row_of(first + j)
                    parts.append(spread(value, y))
                    if build:
                        hots.append(hot_columns(z))
                lane = pl.ds(pl.multiple_of(first * 128, 128), group * 128)
                if build:
                    columns = jnp.concatenate(hots, axis=1)
                    hot[:, lane] = columns
                else:
                    columns = hot[:, lane]
                acc = acc + dot(jnp.concatenate(parts, axis=1), columns, NT)
            return acc

        return total(lax.fori_loop(0, steps, step, jnp.zeros((2 * ROWS, COLS), F32)))

    def sheet_parts(x):
        return jnp.concatenate(split2(x), axis=0).astype(BF16)

    def gather(sheet, first, group, y_of, put):
        lane = pl.ds(pl.multiple_of(first * 128, 128), group * 128)
        got = total(dot(sheet, hot[:, lane], NN))
        for j in range(group):
            here = jnp.where(yrow == y_of(first + j), got[:, j * 128:(j + 1) * 128], 0.0)
            put(first + j, jnp.sum(here, axis=0, keepdims=True))

    pair = math.gcd(2, lines)
    group_p = math.gcd(8, nb)

    @pl.when(jnp.logical_not(solid))
    def _():
        def packet_row(i):
            one = pl.ds(i, 1)
            return link_p[one, :], cell_y[one, :], cell_z[one, :]

        hsum[...] = scatter(nb // group_p, group_p, lambda t: [t * group_p], packet_row, True)

    arrive(a_copies, (0, 1))
    leave(a_copies)
    zr = jnp.concatenate([zst[0], ends(dst8[0], dst8[2], row8n)], axis=0)
    zl = jnp.concatenate([zst[1], ends(dst8[1], dst8[3], row8n)], axis=0)
    lane24 = iota((XR, 128), 1)
    for l in range(LAYERS):
        first_u, last_u = yst[0, l], yst[1, l]
        first_c, last_c = yst[0, LAYERS + l // 2], yst[1, LAYERS + l // 2]
        if l % 2:
            first_c = pltpu.roll(first_c, W, 0)
        else:
            last_c = pltpu.roll(last_c, W, 0)
        pairs = (
            (ua, first_u, pltpu.roll(last_u, W, 0)),
            (rx, pltpu.roll(first_u, W, 0), last_u),
            (cx, first_c, last_c),
        )
        for a, (x, after, prior) in enumerate(pairs):
            x[l, ROWS:XR, 0:COLS] = ends(after, prior, row8)
            g = (l * 3 + a) * W
            right = pltpu.roll(zr, 128 - g, 1) if g else zr
            left = pltpu.roll(zl, 128 - W - 64 - g, 1)
            x[l, :, COLS:XC] = sides(right, left, lane24)

    def sweep(x, y, source):
        for l in range(LAYERS):
            u = x[l]
            left = pltpu.roll(u, 1, 1)
            around = pltpu.roll(u, 1, 0) + pltpu.roll(u, XR - 1, 0) + left + pltpu.roll(u, XC - 1, 1)
            if l > 0:
                around = around + x[l - 1]
            if l < LAYERS - 1:
                around = around + x[l + 1]
            new = u + rx[l] * (around - 6.0 * u) - cx[l] * (u - left)
            if source and l == 0:
                new = new + (sx[0] - gx[0] * u)
            y[l] = new

    def phase(source):
        for repeat in range(SWEEPS // 2):
            sweep(ua, ub, source)
            sweep(ub, ua, source)

    phase(False)

    @pl.when(jnp.logical_not(solid))
    def _():
        sheet = sheet_parts(ua[0, 0:ROWS, 0:COLS])

        def put(i, row):
            q_send[i] = row * link_p[pl.ds(i, 1), :]

        def step(t, _):
            firsts = [far_first(t * pair + a) * wide for a in range(pair)]
            for first in firsts:
                gather(sheet, first, wide, lambda i: cell_y[pl.ds(i, 1), :], put)
            for first in firsts:
                for j in range(wide):
                    pltpu.make_async_remote_copy(
                        src_ref=q_send.at[first + j], dst_ref=q_recv.at[my_row],
                        send_sem=q_ssem, recv_sem=q_rsem.at[my_line],
                        device_id=(last, first + j, slab), device_id_type=MESH,
                    ).start()
            return 0

        lax.fori_loop(0, lines // pair, step, 0)

    begin(u_copies)

    def whole(ref, ssem, rsem):
        return pltpu.make_async_remote_copy(
            src_ref=ref, dst_ref=ref, send_sem=ssem, recv_sem=rsem,
            device_id=neighbour(STEPS[0]), device_id_type=MESH,
        )

    def line_in(t, ref, ssem, rsem):
        line = far_first(lines - 1 - t)
        whole(ref.at[pl.ds(line * deep, deep)], ssem, rsem.at[line]).wait_recv()
        return [line * deep]

    def target_row(i, value):
        code = meta_recv[i, 1:2, :]
        y = jnp.floor(code * (1.0 / 256.0))
        return value, y, code - 256.0 * y

    @pl.when(solid)
    def _():
        for copy in slots:
            copy.wait()
        gx[0, 0:ROWS, 0:COLS] = scatter(
            lines, deep, lambda t: line_in(t, meta_recv, meta_ssem, meta_rsem),
            lambda i: target_row(i, meta_recv[i, 0:1, :]), True,
        )
        begin(g_copies)

    def written(first, count, m):
        return pltpu.make_async_copy(
            ua.at[pl.ds(first, count), pl.ds(0, ROWS), pl.ds(0, COLS)], out.at[pl.ds(first, count)], out_sem.at[m]
        )

    deeper, top = written(1, LAYERS - 1, 0), written(0, 1, 1)

    @pl.when(solid)
    def _():
        sx[0, 0:ROWS, 0:COLS] = scatter(
            lines, deep, lambda t: line_in(t, q_recv, q_ssem, q_rsem), lambda i: target_row(i, q_recv[i]), False
        )
        begin(s_copies)
        finish(u_copies)
        unpack(ua, uy, uz, udg, LAYERS)
        finish(g_copies)
        unpack(gx, gy, gz, gdg, 1)
        g = gx[0]
        inverse = 1.0 / (1.0 + g)
        gx[0] = g * inverse
        finish(s_copies)
        unpack(sx, sy, sz, sdg, 1)
        sx[0] = sx[0] * inverse
        phase(True)
        deeper.start()
        top.start()
        sheet = sheet_parts(ua[0, 0:ROWS, 0:COLS])

        def put(i, row):
            ans_send[i] = row

        def step(t, _):
            to_lines = [far_first(t * pair + a) for a in range(pair)]
            for line in to_lines:
                gather(sheet, line * deep, deep, lambda i: target_row(i, None)[1], put)
            for line in to_lines:
                for j in range(deep):
                    pltpu.make_async_remote_copy(
                        src_ref=ans_send.at[line * deep + j], dst_ref=wall_recv.at[brick],
                        send_sem=ans_ssem, recv_sem=ans_rsem.at[my_line],
                        device_id=(j // wide, line * wide + j % wide, slab), device_id_type=MESH,
                    ).start()
            return 0

        lax.fori_loop(0, lines // pair, step, 0)
        whole(ans_send, ans_ssem, ans_rsem.at[0]).wait_send()

    @pl.when(jnp.logical_not(solid))
    def _():
        finish(u_copies)
        unpack(ua, uy, uz, udg, LAYERS)
        phase(False)
        deeper.start()
        whole(meta_send, meta_ssem, meta_rsem.at[0]).wait_send()
        whole(q_send, q_ssem, q_rsem.at[0]).wait_send()

        def packet_row(i):
            one = pl.ds(i, 1)
            return link_p[one, :] * wall_recv[i], cell_y[one, :], None

        def lines_in(t):
            firsts = []
            for a in range(pair):
                line = far_first(lines - 1 - t * pair - a)
                ref = wall_recv.at[pl.ds(line * wide, wide)]
                whole(ref, ans_ssem, ans_rsem.at[line]).wait_recv()
                firsts.append(line * wide)
            return firsts

        q = scatter(lines // pair, wide, lines_in, packet_row, False)
        h = hsum[...]
        u = ua[0, 0:ROWS, 0:COLS]
        ua[0, 0:ROWS, 0:COLS] = u + (q - h * u) / (1.0 + h)
        top.start()

    deeper.wait()
    top.wait()


def body(nd, nb, ns, heat, ratio, courant, voxel, owner, target, link, tally):
    groups = voxel.size // 128
    slots = [x.reshape(groups, 128) for x in (voxel, owner, target, link)]
    rows_in = (nd - 1) * nb
    most = max(rows_in, nb)
    lines = nb // math.gcd(4, nb)
    vm = pltpu.VMEM
    sem = pltpu.SemaphoreType.DMA

    def stage(layers):
        return [vm((2, layers, 8, COLS), F32), vm((2, layers, ROWS, 128), F32), vm((4, layers, 8, 128), F32)]

    field = vm((LAYERS, XR, XC), F32)
    scratch = (
        [field] * 4 + [vm((1, XR, XC), F32)] * 2
        + [vm((groups, 128), I32)] * 3 + [vm((groups, 128), F32), vm((1, 1, 1), I32)]
        + [vm((2, LAYERS + 2, 8, COLS), F32), vm((ROWS, 128), F32)]
        + [vm((2, LAYERS + 2, 8, COLS), F32), vm((2, ROWS, 128), F32), vm((4, 8, 128), F32)]
        + stage(LAYERS) + stage(1) + stage(1)
        + [vm((COLS, most * CAP), BF16), vm((groups * nb, 128), F32), vm((groups * nb, 256), F32)]
        + [vm((PARTS * nb, groups * 128), BF16), vm((128, groups * 128), BF16)]
        + [vm((nb, CAP), F32)] * 3 + [vm((ROWS, COLS), F32)]
        + [vm((nb, 2, CAP), F32), vm((nb, 1, CAP), F32), vm((rows_in, 2, CAP), F32), vm((rows_in, 1, CAP), F32)]
        + [vm((rows_in, 1, CAP), F32), vm((nb, 1, CAP), F32)]
        + [sem((3,)), sem((5,)), sem((2,))]
        + [sem((8,))] * 8
        + [pltpu.SemaphoreType.REGULAR] + [sem, sem((lines,))] * 3
    )
    hbm = pl.BlockSpec(memory_space=pl.ANY)
    return pl.pallas_call(
        functools.partial(kernel, nd, nb, ns),
        out_shape=jax.ShapeDtypeStruct(heat.shape, F32),
        in_specs=[hbm] * 8,
        out_specs=hbm,
        scratch_shapes=scratch,
        compiler_params=pltpu.CompilerParams(
            collective_id=0, has_side_effects=True, vmem_limit_bytes=VMEM_BYTES
        ),
    )(heat, ratio, courant, *slots, tally)


def solution(mesh):
    nd, nb, ns = (mesh.shape[a] for a in ("dom", "brick", "slab"))
    where = P("dom", "brick", "slab")
    return jax.shard_map(
        functools.partial(body, nd, nb, ns),
        mesh=mesh,
        in_specs=(where,) * 8,
        out_specs=where,
        check_vma=False,
    )
```

```python
import functools
import math

import jax
import jax.numpy as jnp
from jax import lax
from jax.experimental import pallas as pl
from jax.experimental.pallas import tpu as pltpu
from jax.sharding import PartitionSpec as P

SWEEPS = 4
W = 4
HIGH, LOW = 32, 128
CAP = 128
VMEM_BYTES = 60 * 1024 * 1024
LAYERS, ROWS, COLS = 4, 16, 256
XR, XC = ROWS + 8, COLS + 128
PARTS = 7
STEPS = ((-1, 0), (1, 0), (0, -1), (0, 1), (-1, -1), (-1, 1), (1, -1), (1, 1))
DOWN = (0, -1)
MESH = pl.DeviceIdType.MESH
F32, BF16, I32 = jnp.float32, jnp.bfloat16, jnp.int32
NT = (((1,), (1,)), ((), ()))
NN = (((1,), (0,)), ((), ()))


def iota(shape, dim):
    return lax.broadcasted_iota(I32, shape, dim)


def dot(a, b, dims):
    return lax.dot_general(a, b, dims, preferred_element_type=F32)


def split2(x):
    high = x.astype(BF16).astype(F32)
    return high, x - high


def kernel(
    nd, nb, ns,
    heat, ratio, courant, voxel_h, owner_h, target_h, link_h, tally_h,
    out,
    ua, ub, rx, cx, gx, sx,
    voxel, owner, target, link, tally,
    ysend, zsend, yst, zst, dst8,
    uys, uzs, uy, uz, udg, gy, gz, gdg, sy, sz, sdg,
    hot, owner_hot, prefix, meta_a, meta_b,
    cell_high, cell_low, link_p, hsum,
    meta_send, q_send, meta_recv, q_recv, ans_send, wall_recv,
    in_sem, slot_sem,
    a_send, a_recv, u_send, u_recv, g_send, g_recv, s_send, s_recv,
    ready, meta_ssem, meta_rsem, q_ssem, q_rsem, ans_ssem, ans_rsem,
):
    dom, brick, slab = lax.axis_index("dom"), lax.axis_index("brick"), lax.axis_index("slab")
    last = nd - 1
    solid = dom == last
    rows_in = last * nb
    wide = math.gcd(4, nb)
    lines = nb // wide
    deep = last * wide
    my_line, my_place = lax.div(brick, wide), lax.rem(brick, wide)
    my_row = my_line * deep + dom * wide + my_place

    def far_first(t):
        k = lax.div(t + 1, 2)
        away = lines // 2 + jnp.where(lax.rem(t, 2) == 0, k, -k)
        return lax.rem(my_line + away + lines, lines)

    own = (slice(None), pl.ds(0, ROWS), pl.ds(0, COLS))
    fields = [
        pltpu.make_async_copy(h, x.at[own], in_sem.at[i])
        for i, (h, x) in enumerate(((heat, ua), (ratio, rx), (courant, cx)))
    ]
    slots = [
        pltpu.make_async_copy(h, v, slot_sem.at[i])
        for i, (h, v) in enumerate(((owner_h, owner), (voxel_h, voxel), (target_h, target), (link_h, link), (tally_h, tally)))
    ]

    def neighbour(step):
        db, dz = step
        return (dom, lax.rem(brick + db + nb, nb), lax.rem(slab + dz + ns, ns))

    def exists(step):
        db, dz = step
        b, z = brick + db, slab + dz
        return (b >= 0) & (b < nb) & (z >= 0) & (z < ns)

    def on(step, act):
        pl.when(exists(step))(act)

    barrier = pltpu.get_barrier_semaphore()

    def greet(*device):
        pl.semaphore_signal(barrier, inc=1, device_id=device, device_id_type=MESH)

    for step in STEPS:
        if step[1] >= 0:

            @functools.partial(on, step)
            def _():
                greet(*neighbour(step))

    @pl.when(solid)
    def _():
        def other(i, _):
            greet(last, lax.rem(my_line + i, lines) * wide + my_place, slab)
            return 0

        lax.fori_loop(1, lines, other, 0)

    @pl.when(jnp.logical_not(solid))
    def _():
        for j in range(wide):
            greet(last, my_line * wide + j, slab)

    for copy in fields:
        copy.start()
    for copy in slots:
        copy.start()

    gas = jnp.where(solid, 0.0, 1.0).astype(F32)
    rows_end = jnp.where(brick < nb - 1, W, 0)
    rows_from = jnp.where(brick > 0, 8 - W, 8)
    lanes_end = jnp.where(slab < ns - 1, W, 0)
    lanes_from = jnp.where(slab > 0, 128 - W, 128)

    for copy in fields:
        copy.wait()
    lane16 = iota((ROWS, 128), 1)

    def pack(planes, rows, columns):
        packed = jnp.zeros((ROWS, 128), F32)
        for g, x in enumerate(planes):
            half = slice(g % 2 * W, g % 2 * W + W)
            rows[0, g // 2, half, :] = x[0:W]
            rows[1, g // 2, half, :] = x[ROWS - W:]
            at = g * W
            head = pltpu.roll(x[:, 0:128], at, 1) if g else x[:, 0:128]
            tail = pltpu.roll(x[:, 128:256], (64 + at + W) % 128, 1)
            packed = jnp.where((lane16 >= at) & (lane16 < at + W), head, packed)
            packed = jnp.where((lane16 >= 64 + at) & (lane16 < 64 + at + W), tail, packed)
        columns[...] = packed

    def plane(x, l):
        return x[l, 0:ROWS, 0:COLS]

    for l in range(LAYERS):
        cx[l, 0:ROWS, 0:COLS] = plane(cx, l) * gas
    pack([plane(x, l) for l in range(LAYERS) for x in (ua, rx, cx)], ysend, zsend)

    beside = sum(jnp.where(exists(step), 1, 0) for step in STEPS if step[1] <= 0)
    pl.semaphore_wait(barrier, beside + jnp.where(solid, deep + lines - 1, 0))

    @pl.when(solid)
    def _():
        for d in range(last):
            for j in range(wide):
                pl.semaphore_signal(ready, inc=1, device_id=(d, my_line * wide + j, slab), device_id_type=MESH)

    def halo_copies(sources, landings, ssem, rsem):
        return [
            pltpu.make_async_remote_copy(
                src_ref=sources[m], dst_ref=landings[m], send_sem=ssem.at[m], recv_sem=rsem.at[m],
                device_id=neighbour(step), device_id_type=MESH,
            )
            for m, step in enumerate(STEPS)
        ]

    everywhere = (-1, 0, 1)

    def begin(copies, ways=everywhere):
        for m in reversed(range(len(STEPS))):
            if STEPS[m][1] in ways:
                on(STEPS[m], copies[m].start)

    def arrive(copies, steps=STEPS):
        for db, dz in steps:
            on((-db, -dz), copies[STEPS.index((db, dz))].wait_recv)

    def leave(copies):
        for step, copy in zip(STEPS, copies):
            on(step, copy.wait_send)

    def finish(copies):
        arrive(copies)
        leave(copies)

    def packed_copies(rows, columns, y, z, d, ssem, rsem):
        head, tail = columns.at[pl.ds(0, 8)], columns.at[pl.ds(ROWS - 8, 8)]
        return halo_copies(
            [rows.at[0], rows.at[1], columns, columns, head, head, tail, tail],
            [y.at[0], y.at[1], z.at[0], z.at[1]] + [d.at[i] for i in range(4)],
            ssem, rsem,
        )

    a_copies = packed_copies(ysend, zsend, yst, zst, dst8, a_send, a_recv)
    begin(a_copies, (-1, 0))

    def high_of(cell):
        return (((cell >> 7) & 1) * ROWS + (cell >> 8)).astype(F32)

    @pl.when(jnp.logical_not(solid))
    def _():
        for copy in slots:
            copy.wait()
        live_count = tally[0]
        a, b = iota((128, 128), 0), iota((128, 128), 1)
        before = jnp.concatenate([jnp.where(a < b, 1.0, 0.0), jnp.ones((128, 128), F32)], axis=1).astype(BF16)
        bricks = iota((nb, 128), 0)
        lanes = iota((1, 128), 1)
        groups = owner.shape[0]

        def mark(j, _):
            live = j * 128 + lanes < live_count
            named = jnp.where(live, owner[pl.ds(j, 1), :], nb)
            owner_hot[pl.ds(pl.multiple_of(j * nb, nb), nb), :] = jnp.where(bricks == named, 1.0, 0.0)
            return 0

        lax.fori_loop(0, groups, mark, 0)
        prefix[...] = dot(owner_hot[...].astype(BF16), before, NN)

        def lay(j, carry):
            at = pl.ds(pl.multiple_of(j * nb, nb), nb)
            lane = pl.ds(pl.multiple_of(j * 128, 128), 128)
            one = owner_hot[at, :]
            rank = jnp.sum(one * (prefix[at, 0:128] + carry), axis=0, keepdims=True)
            meta_b[:, lane] = jnp.where(iota((128, 128), 0).astype(F32) == rank, 1.0, 0.0).astype(BF16)
            v, t = voxel[pl.ds(j, 1), :], target[pl.ds(j, 1), :]
            k = link[pl.ds(j, 1), :]
            k1, rest = split2(k)
            k2, k3 = split2(rest)
            values = (
                high_of(v), (v & (LOW - 1)).astype(F32), high_of(t), (t & (LOW - 1)).astype(F32),
                k1, k2, k3,
            )
            for q, value in enumerate(values):
                meta_a[q * nb:(q + 1) * nb, lane] = (one * value).astype(BF16)
            return carry + prefix[at, 128:256]

        lax.fori_loop(0, groups, lay, jnp.zeros((nb, 128), F32))
        packet = dot(meta_a[...], meta_b[...], NT)
        part = [packet[q * nb:(q + 1) * nb] for q in range(PARTS)]
        cell_high[...], cell_low[...] = part[0], part[1]
        code = part[2] * float(LOW) + part[3]
        k = part[4] + part[5] + part[6]
        link_p[...] = k
        for o in range(nb):
            meta_send[o, 0:1, :] = k[o:o + 1]
            meta_send[o, 1:2, :] = code[o:o + 1]

    def sheet_copies(x, y, z, d, ssem, rsem):
        def part(r0, rn, c0, cn):
            return x.at[:, pl.ds(r0, rn), pl.ds(c0, cn)]

        return halo_copies(
            [
                part(0, 8, 0, COLS), part(ROWS - 8, 8, 0, COLS),
                part(0, ROWS, 0, 128), part(0, ROWS, COLS - 128, 128),
                part(0, 8, 0, 128), part(0, 8, COLS - 128, 128),
                part(ROWS - 8, 8, 0, 128), part(ROWS - 8, 8, COLS - 128, 128),
            ],
            [y.at[0], y.at[1], z.at[0], z.at[1]] + [d.at[i] for i in range(4)],
            ssem, rsem,
        )

    u_copies = packed_copies(uys, uzs, uy, uz, udg, u_send, u_recv)
    g_copies = sheet_copies(gx, gy, gz, gdg, g_send, g_recv)
    s_copies = sheet_copies(sx, sy, sz, sdg, s_send, s_recv)

    row8 = iota((8, COLS), 0)
    row8n = iota((8, 128), 0)
    lane8 = iota((8, 128), 1)

    def sides(right, left, lanes):
        return jnp.where(lanes < lanes_end, right, jnp.where(lanes >= lanes_from, left, 0.0))

    def ends(after, prior, rows):
        return jnp.where(rows < rows_end, after, jnp.where(rows >= rows_from, prior, 0.0))

    def unpack_sheet(x, y, z, d):
        x[0, ROWS:XR, 0:COLS] = ends(y[0, 0], y[1, 0], row8)
        x[0, 0:ROWS, COLS:XC] = sides(z[0, 0], z[1, 0], lane16)
        right = ends(d[0, 0], d[2, 0], row8n)
        left = ends(d[1, 0], d[3, 0], row8n)
        x[0, ROWS:XR, COLS:XC] = sides(right, left, lane8)

    lane24 = iota((XR, 128), 1)

    def unpack(planes, y, z, d):
        right = jnp.concatenate([z[0], ends(d[0], d[2], row8n)], axis=0)
        left = jnp.concatenate([z[1], ends(d[1], d[3], row8n)], axis=0)
        for g, (x, l) in enumerate(planes):
            after, prior = y[0, g // 2], y[1, g // 2]
            if g % 2:
                after = pltpu.roll(after, W, 0)
            else:
                prior = pltpu.roll(prior, W, 0)
            x[l, ROWS:XR, 0:COLS] = ends(after, prior, row8)
            at = g * W
            x[l, :, COLS:XC] = sides(
                pltpu.roll(right, 128 - at, 1) if g else right, pltpu.roll(left, 64 - W - at, 1), lane24
            )

    arrive(a_copies, [DOWN])
    begin(a_copies, (1,))

    low_row = iota((LOW, 128), 0).astype(F32)
    high_row = iota((HIGH, 128), 0).astype(F32)

    def hot_columns(at_low):
        return jnp.where(low_row == at_low, 1.0, 0.0).astype(BF16)

    def spread(value, at_high):
        a, b = split2(value)
        there = high_row == at_high
        return jnp.concatenate([jnp.where(there, a, 0.0), jnp.where(there, b, 0.0)], axis=0).astype(BF16)

    def total(x):
        return x[0:HIGH] + x[HIGH:2 * HIGH]

    def scatter(steps, group, blocks_of, row_of, build):
        def step(t, acc):
            blocks = blocks_of(t)
            for first in blocks:
                parts, hots = [], []
                for j in range(group):
                    value, at_high, at_low = row_of(first + j)
                    parts.append(spread(value, at_high))
                    if build:
                        hots.append(hot_columns(at_low))
                lane = pl.ds(pl.multiple_of(first * 128, 128), group * 128)
                if build:
                    columns = jnp.concatenate(hots, axis=1)
                    hot[:, lane] = columns
                else:
                    columns = hot[:, lane]
                acc = acc + dot(jnp.concatenate(parts, axis=1), columns, NT)
            return acc

        sums = total(lax.fori_loop(0, steps, step, jnp.zeros((2 * HIGH, LOW), F32)))
        return jnp.concatenate([sums[0:ROWS], sums[ROWS:HIGH]], axis=1)

    def sheet_parts(x):
        x = jnp.concatenate([x[:, 0:LOW], x[:, LOW:COLS]], axis=0)
        return jnp.concatenate(split2(x), axis=0).astype(BF16)

    def gather(sheet, first, group, high_at, put):
        lane = pl.ds(pl.multiple_of(first * 128, 128), group * 128)
        got = total(dot(sheet, hot[:, lane], NN))
        for j in range(group):
            here = jnp.where(high_row == high_at(first + j), got[:, j * 128:(j + 1) * 128], 0.0)
            put(first + j, jnp.sum(here, axis=0, keepdims=True))

    pair = math.gcd(2, lines)
    group_p = math.gcd(8, nb)

    @pl.when(jnp.logical_not(solid))
    def _():
        def packet_row(i):
            one = pl.ds(i, 1)
            return link_p[one, :], cell_high[one, :], cell_low[one, :]

        hsum[...] = scatter(nb // group_p, group_p, lambda t: [t * group_p], packet_row, True)

    @pl.when(jnp.logical_not(solid))
    def _():
        pl.semaphore_wait(ready, wide)

        def send(i, _):
            to = far_first(lax.div(i, wide)) * wide + lax.rem(i, wide)
            pltpu.make_async_remote_copy(
                src_ref=meta_send.at[to], dst_ref=meta_recv.at[my_row],
                send_sem=meta_ssem, recv_sem=meta_rsem.at[my_line], device_id=(last, to, slab), device_id_type=MESH,
            ).start()
            return 0

        lax.fori_loop(0, nb, send, 0)

    arrive(a_copies, [step for step in STEPS if step != DOWN])
    leave(a_copies)
    unpack([(x, l) for l in range(LAYERS) for x in (ua, rx, cx)], yst, zst, dst8)

    def sweep(x, y, source):
        for l in range(LAYERS):
            u = x[l]
            left = pltpu.roll(u, 1, 1)
            around = pltpu.roll(u, 1, 0) + pltpu.roll(u, XR - 1, 0) + left + pltpu.roll(u, XC - 1, 1)
            if l > 0:
                around = around + x[l - 1]
            if l < LAYERS - 1:
                around = around + x[l + 1]
            new = u + rx[l] * (around - 6.0 * u) - cx[l] * (u - left)
            if source and l == 0:
                new = new + (sx[0] - gx[0] * u)
            y[l] = new

    def phase(source):
        for repeat in range(SWEEPS // 2):
            sweep(ua, ub, source)
            sweep(ub, ua, source)

    phase(False)

    @pl.when(jnp.logical_not(solid))
    def _():
        sheet = sheet_parts(ua[0, 0:ROWS, 0:COLS])

        def put(i, row):
            q_send[i] = row * link_p[pl.ds(i, 1), :]

        def step(t, _):
            firsts = [far_first(t * pair + a) * wide for a in range(pair)]
            for first in firsts:
                gather(sheet, first, wide, lambda i: cell_high[pl.ds(i, 1), :], put)
            for first in firsts:
                for j in range(wide):
                    pltpu.make_async_remote_copy(
                        src_ref=q_send.at[first + j], dst_ref=q_recv.at[my_row],
                        send_sem=q_ssem, recv_sem=q_rsem.at[my_line],
                        device_id=(last, first + j, slab), device_id_type=MESH,
                    ).start()
            return 0

        lax.fori_loop(0, lines // pair, step, 0)

    pack([plane(ua, l) for l in range(LAYERS)], uys, uzs)
    begin(u_copies)

    def whole(ref, ssem, rsem):
        return pltpu.make_async_remote_copy(
            src_ref=ref, dst_ref=ref, send_sem=ssem, recv_sem=rsem,
            device_id=neighbour(STEPS[0]), device_id_type=MESH,
        )

    def line_in(t, ref, ssem, rsem):
        line = far_first(lines - 1 - t)
        whole(ref.at[pl.ds(line * deep, deep)], ssem, rsem.at[line]).wait_recv()
        return [line * deep]

    def target_row(i, value):
        code = meta_recv[i, 1:2, :]
        high = jnp.floor(code * (1.0 / LOW))
        return value, high, code - float(LOW) * high

    @pl.when(solid)
    def _():
        for copy in slots:
            copy.wait()
        gx[0, 0:ROWS, 0:COLS] = scatter(
            lines, deep, lambda t: line_in(t, meta_recv, meta_ssem, meta_rsem),
            lambda i: target_row(i, meta_recv[i, 0:1, :]), True,
        )
        begin(g_copies)

    @pl.when(solid)
    def _():
        sx[0, 0:ROWS, 0:COLS] = scatter(
            lines, deep, lambda t: line_in(t, q_recv, q_ssem, q_rsem), lambda i: target_row(i, q_recv[i]), False
        )
        begin(s_copies)
        finish(u_copies)
        unpack([(ua, l) for l in range(LAYERS)], uy, uz, udg)
        finish(g_copies)
        unpack_sheet(gx, gy, gz, gdg)
        g = gx[0]
        inverse = 1.0 / (1.0 + g)
        gx[0] = g * inverse
        finish(s_copies)
        unpack_sheet(sx, sy, sz, sdg)
        sx[0] = sx[0] * inverse
        phase(True)
        for l in range(LAYERS):
            out[l] = plane(ua, l)
        sheet = sheet_parts(ua[0, 0:ROWS, 0:COLS])

        def put(i, row):
            ans_send[i] = row

        def step(t, _):
            to_lines = [far_first(t * pair + a) for a in range(pair)]
            for line in to_lines:
                gather(sheet, line * deep, deep, lambda i: target_row(i, None)[1], put)
            for line in to_lines:
                for j in range(deep):
                    pltpu.make_async_remote_copy(
                        src_ref=ans_send.at[line * deep + j], dst_ref=wall_recv.at[brick],
                        send_sem=ans_ssem, recv_sem=ans_rsem.at[my_line],
                        device_id=(j // wide, line * wide + j % wide, slab), device_id_type=MESH,
                    ).start()
            return 0

        lax.fori_loop(0, lines // pair, step, 0)
        whole(ans_send, ans_ssem, ans_rsem.at[0]).wait_send()

    @pl.when(jnp.logical_not(solid))
    def _():
        finish(u_copies)
        unpack([(ua, l) for l in range(LAYERS)], uy, uz, udg)
        phase(False)
        for l in range(1, LAYERS):
            out[l] = plane(ua, l)
        whole(meta_send, meta_ssem, meta_rsem.at[0]).wait_send()
        whole(q_send, q_ssem, q_rsem.at[0]).wait_send()

        def packet_row(i):
            one = pl.ds(i, 1)
            return link_p[one, :] * wall_recv[i], cell_high[one, :], None

        def lines_in(t):
            firsts = []
            for a in range(pair):
                line = far_first(lines - 1 - t * pair - a)
                ref = wall_recv.at[pl.ds(line * wide, wide)]
                whole(ref, ans_ssem, ans_rsem.at[line]).wait_recv()
                firsts.append(line * wide)
            return firsts

        q = scatter(lines // pair, wide, lines_in, packet_row, False)
        h = hsum[...]
        u = ua[0, 0:ROWS, 0:COLS]
        out[0] = u + (q - h * u) / (1.0 + h)


def body(nd, nb, ns, heat, ratio, courant, voxel, owner, target, link, tally):
    groups = voxel.size // 128
    slots = [x.reshape(groups, 128) for x in (voxel, owner, target, link)]
    rows_in = (nd - 1) * nb
    most = max(rows_in, nb)
    lines = nb // math.gcd(4, nb)
    vm = pltpu.VMEM
    sem = pltpu.SemaphoreType.DMA

    def landings(planes):
        return [vm((2, planes // 2, 8, COLS), F32), vm((2, ROWS, 128), F32), vm((4, 8, 128), F32)]

    def packing(planes):
        return [vm((2, planes // 2, 8, COLS), F32), vm((ROWS, 128), F32)]

    sheet = [vm((2, 1, 8, COLS), F32), vm((2, 1, ROWS, 128), F32), vm((4, 1, 8, 128), F32)]

    field = vm((LAYERS, XR, XC), F32)
    scratch = (
        [field] * 4 + [vm((1, XR, XC), F32)] * 2
        + [vm((groups, 128), I32)] * 3 + [vm((groups, 128), F32), vm((1, 1, 1), I32)]
        + packing(3 * LAYERS) + landings(3 * LAYERS) + packing(LAYERS) + landings(LAYERS) + sheet * 2
        + [vm((LOW, most * CAP), BF16), vm((groups * nb, 128), F32), vm((groups * nb, 256), F32)]
        + [vm((PARTS * nb, groups * 128), BF16), vm((128, groups * 128), BF16)]
        + [vm((nb, CAP), F32)] * 3 + [vm((ROWS, COLS), F32)]
        + [vm((nb, 2, CAP), F32), vm((nb, 1, CAP), F32), vm((rows_in, 2, CAP), F32), vm((rows_in, 1, CAP), F32)]
        + [vm((rows_in, 1, CAP), F32), vm((nb, 1, CAP), F32)]
        + [sem((3,)), sem((5,))]
        + [sem((8,))] * 8
        + [pltpu.SemaphoreType.REGULAR] + [sem, sem((lines,))] * 3
    )
    hbm = pl.BlockSpec(memory_space=pl.ANY)
    return pl.pallas_call(
        functools.partial(kernel, nd, nb, ns),
        out_shape=pltpu.VMEM(heat.shape, F32),
        in_specs=[hbm] * 8,
        out_specs=pl.BlockSpec(memory_space=pltpu.VMEM),
        scratch_shapes=scratch,
        compiler_params=pltpu.CompilerParams(
            collective_id=0, has_side_effects=True, vmem_limit_bytes=VMEM_BYTES
        ),
    )(heat, ratio, courant, *slots, tally)


def solution(mesh):
    nd, nb, ns = (mesh.shape[a] for a in ("dom", "brick", "slab"))
    where = P("dom", "brick", "slab")
    return jax.shard_map(
        functools.partial(body, nd, nb, ns),
        mesh=mesh,
        in_specs=(where,) * 8,
        out_specs=where,
        check_vma=False,
    )
```

```python
import functools
import math

import jax
import jax.numpy as jnp
from jax import lax
from jax.experimental import pallas as pl
from jax.experimental.pallas import tpu as pltpu
from jax.sharding import PartitionSpec as P

SWEEPS = 4
W = 4
HIGH, LOW = 32, 128
CAP = 128
VMEM_BYTES = 60 * 1024 * 1024
LAYERS, ROWS, COLS = 4, 16, 256
XR, XC = ROWS + 8, COLS + 128
PARTS = 7
STEPS = ((-1, 0), (1, 0), (0, -1), (0, 1), (-1, -1), (-1, 1), (1, -1), (1, 1))
DOWN = (0, -1)
MESH = pl.DeviceIdType.MESH
F32, BF16, I32 = jnp.float32, jnp.bfloat16, jnp.int32
NT = (((1,), (1,)), ((), ()))
NN = (((1,), (0,)), ((), ()))


def iota(shape, dim):
    return lax.broadcasted_iota(I32, shape, dim)


def dot(a, b, dims):
    return lax.dot_general(a, b, dims, preferred_element_type=F32)


def split2(x):
    high = x.astype(BF16).astype(F32)
    return high, x - high


def kernel(
    nd, nb, ns,
    heat, ratio, courant, voxel_h, owner_h, target_h, link_h, tally_h,
    out,
    ua, ub, rx, cx, gx, sx,
    voxel, owner, target, link, tally,
    ysend, zsend, yst, zst, dst8,
    uys, uzs, uy, uz, udg, gy, gz, gdg, sy, sz, sdg,
    hot, owner_hot, prefix, meta_a, meta_b,
    cell_high, cell_low, link_p, hsum,
    meta_send, q_send, meta_recv, q_recv, ans_send, wall_recv,
    in_sem, slot_sem,
    a_send, a_recv, u_send, u_recv, g_send, g_recv, s_send, s_recv,
    ready, meta_ssem, meta_rsem, q_ssem, q_rsem, ans_ssem, ans_rsem,
):
    dom, brick, slab = lax.axis_index("dom"), lax.axis_index("brick"), lax.axis_index("slab")
    last = nd - 1
    solid = dom == last
    rows_in = last * nb
    wide = math.gcd(4, nb)
    lines = nb // wide
    deep = last * wide
    my_line, my_place = lax.div(brick, wide), lax.rem(brick, wide)
    my_row = my_line * deep + dom * wide + my_place

    def far_first(t):
        k = lax.div(t + 1, 2)
        away = lines // 2 + jnp.where(lax.rem(t, 2) == 0, k, -k)
        return lax.rem(my_line + away + lines, lines)

    own = (slice(None), pl.ds(0, ROWS), pl.ds(0, COLS))
    fields = [
        pltpu.make_async_copy(h, x.at[own], in_sem.at[i])
        for i, (h, x) in enumerate(((heat, ua), (ratio, rx), (courant, cx)))
    ]
    slots = [
        pltpu.make_async_copy(h, v, slot_sem.at[i])
        for i, (h, v) in enumerate(((owner_h, owner), (voxel_h, voxel), (target_h, target), (link_h, link), (tally_h, tally)))
    ]

    def neighbour(step):
        db, dz = step
        return (dom, lax.rem(brick + db + nb, nb), lax.rem(slab + dz + ns, ns))

    def exists(step):
        db, dz = step
        b, z = brick + db, slab + dz
        return (b >= 0) & (b < nb) & (z >= 0) & (z < ns)

    def on(step, act):
        pl.when(exists(step))(act)

    barrier = pltpu.get_barrier_semaphore()

    def greet(*device):
        pl.semaphore_signal(barrier, inc=1, device_id=device, device_id_type=MESH)

    for step in STEPS:
        if step[1] >= 0:

            @functools.partial(on, step)
            def _():
                greet(*neighbour(step))

    @pl.when(solid)
    def _():
        def other(i, _):
            greet(last, lax.rem(my_line + i, lines) * wide + my_place, slab)
            return 0

        lax.fori_loop(1, lines, other, 0)

    @pl.when(jnp.logical_not(solid))
    def _():
        for j in range(wide):
            greet(last, my_line * wide + j, slab)

    for copy in fields:
        copy.start()
    for copy in slots:
        copy.start()

    gas = jnp.where(solid, 0.0, 1.0).astype(F32)
    rows_end = jnp.where(brick < nb - 1, W, 0)
    rows_from = jnp.where(brick > 0, 8 - W, 8)
    lanes_end = jnp.where(slab < ns - 1, W, 0)
    lanes_from = jnp.where(slab > 0, 128 - W, 128)

    for copy in fields:
        copy.wait()
    lane16 = iota((ROWS, 128), 1)

    def pack(planes, rows, columns):
        packed = jnp.zeros((ROWS, 128), F32)
        for g, x in enumerate(planes):
            half = slice(g % 2 * W, g % 2 * W + W)
            rows[0, g // 2, half, :] = x[0:W]
            rows[1, g // 2, half, :] = x[ROWS - W:]
            at = g * W
            head = pltpu.roll(x[:, 0:128], at, 1) if g else x[:, 0:128]
            tail = pltpu.roll(x[:, 128:256], (64 + at + W) % 128, 1)
            packed = jnp.where((lane16 >= at) & (lane16 < at + W), head, packed)
            packed = jnp.where((lane16 >= 64 + at) & (lane16 < 64 + at + W), tail, packed)
        columns[...] = packed

    def plane(x, l):
        return x[l, 0:ROWS, 0:COLS]

    for l in range(LAYERS):
        cx[l, 0:ROWS, 0:COLS] = plane(cx, l) * gas
    pack([plane(x, l) for l in range(LAYERS) for x in (ua, rx, cx)], ysend, zsend)

    beside = sum(jnp.where(exists(step), 1, 0) for step in STEPS if step[1] <= 0)
    pl.semaphore_wait(barrier, beside + jnp.where(solid, deep + lines - 1, 0))

    @pl.when(solid)
    def _():
        for d in range(last):
            for j in range(wide):
                pl.semaphore_signal(ready, inc=1, device_id=(d, my_line * wide + j, slab), device_id_type=MESH)

    def halo_copies(sources, landings, ssem, rsem):
        return [
            pltpu.make_async_remote_copy(
                src_ref=sources[m], dst_ref=landings[m], send_sem=ssem.at[m], recv_sem=rsem.at[m],
                device_id=neighbour(step), device_id_type=MESH,
            )
            for m, step in enumerate(STEPS)
        ]

    everywhere = (-1, 0, 1)

    def begin(copies, ways=everywhere):
        for m in reversed(range(len(STEPS))):
            if STEPS[m][1] in ways:
                on(STEPS[m], copies[m].start)

    def arrive(copies, steps=STEPS):
        for db, dz in steps:
            on((-db, -dz), copies[STEPS.index((db, dz))].wait_recv)

    def leave(copies):
        for step, copy in zip(STEPS, copies):
            on(step, copy.wait_send)

    def finish(copies):
        arrive(copies)
        leave(copies)

    def packed_copies(rows, columns, y, z, d, ssem, rsem):
        head, tail = columns.at[pl.ds(0, 8)], columns.at[pl.ds(ROWS - 8, 8)]
        return halo_copies(
            [rows.at[0], rows.at[1], columns, columns, head, head, tail, tail],
            [y.at[0], y.at[1], z.at[0], z.at[1]] + [d.at[i] for i in range(4)],
            ssem, rsem,
        )

    a_copies = packed_copies(ysend, zsend, yst, zst, dst8, a_send, a_recv)
    begin(a_copies, (-1, 0))

    def high_of(cell):
        return (((cell >> 7) & 1) * ROWS + (cell >> 8)).astype(F32)

    @pl.when(jnp.logical_not(solid))
    def _():
        for copy in slots:
            copy.wait()
        live_count = tally[0]
        a, b = iota((128, 128), 0), iota((128, 128), 1)
        before = jnp.concatenate([jnp.where(a < b, 1.0, 0.0), jnp.ones((128, 128), F32)], axis=1).astype(BF16)
        bricks = iota((nb, 128), 0)
        lanes = iota((1, 128), 1)
        groups = owner.shape[0]

        def mark(j, _):
            live = j * 128 + lanes < live_count
            named = jnp.where(live, owner[pl.ds(j, 1), :], nb)
            owner_hot[pl.ds(pl.multiple_of(j * nb, nb), nb), :] = jnp.where(bricks == named, 1.0, 0.0)
            return 0

        lax.fori_loop(0, groups, mark, 0)
        prefix[...] = dot(owner_hot[...].astype(BF16), before, NN)

        def lay(j, carry):
            at = pl.ds(pl.multiple_of(j * nb, nb), nb)
            lane = pl.ds(pl.multiple_of(j * 128, 128), 128)
            one = owner_hot[at, :]
            rank = jnp.sum(one * (prefix[at, 0:128] + carry), axis=0, keepdims=True)
            meta_b[:, lane] = jnp.where(iota((128, 128), 0).astype(F32) == rank, 1.0, 0.0).astype(BF16)
            v, t = voxel[pl.ds(j, 1), :], target[pl.ds(j, 1), :]
            k = link[pl.ds(j, 1), :]
            k1, rest = split2(k)
            k2, k3 = split2(rest)
            values = (
                high_of(v), (v & (LOW - 1)).astype(F32), high_of(t), (t & (LOW - 1)).astype(F32),
                k1, k2, k3,
            )
            for q, value in enumerate(values):
                meta_a[q * nb:(q + 1) * nb, lane] = (one * value).astype(BF16)
            return carry + prefix[at, 128:256]

        lax.fori_loop(0, groups, lay, jnp.zeros((nb, 128), F32))
        packet = dot(meta_a[...], meta_b[...], NT)
        part = [packet[q * nb:(q + 1) * nb] for q in range(PARTS)]
        cell_high[...], cell_low[...] = part[0], part[1]
        code = part[2] * float(LOW) + part[3]
        k = part[4] + part[5] + part[6]
        link_p[...] = k
        for o in range(nb):
            meta_send[o, 0:1, :] = k[o:o + 1]
            meta_send[o, 1:2, :] = code[o:o + 1]

    def sheet_copies(x, y, z, d, ssem, rsem):
        def part(r0, rn, c0, cn):
            return x.at[:, pl.ds(r0, rn), pl.ds(c0, cn)]

        return halo_copies(
            [
                part(0, 8, 0, COLS), part(ROWS - 8, 8, 0, COLS),
                part(0, ROWS, 0, 128), part(0, ROWS, COLS - 128, 128),
                part(0, 8, 0, 128), part(0, 8, COLS - 128, 128),
                part(ROWS - 8, 8, 0, 128), part(ROWS - 8, 8, COLS - 128, 128),
            ],
            [y.at[0], y.at[1], z.at[0], z.at[1]] + [d.at[i] for i in range(4)],
            ssem, rsem,
        )

    u_copies = packed_copies(uys, uzs, uy, uz, udg, u_send, u_recv)
    g_copies = sheet_copies(gx, gy, gz, gdg, g_send, g_recv)
    s_copies = sheet_copies(sx, sy, sz, sdg, s_send, s_recv)

    row8 = iota((8, COLS), 0)
    row8n = iota((8, 128), 0)
    lane8 = iota((8, 128), 1)

    def sides(right, left, lanes):
        return jnp.where(lanes < lanes_end, right, jnp.where(lanes >= lanes_from, left, 0.0))

    def ends(after, prior, rows):
        return jnp.where(rows < rows_end, after, jnp.where(rows >= rows_from, prior, 0.0))

    def unpack_sheet(x, y, z, d):
        x[0, ROWS:XR, 0:COLS] = ends(y[0, 0], y[1, 0], row8)
        x[0, 0:ROWS, COLS:XC] = sides(z[0, 0], z[1, 0], lane16)
        right = ends(d[0, 0], d[2, 0], row8n)
        left = ends(d[1, 0], d[3, 0], row8n)
        x[0, ROWS:XR, COLS:XC] = sides(right, left, lane8)

    lane24 = iota((XR, 128), 1)

    def unpack(planes, y, z, d):
        right = jnp.concatenate([z[0], ends(d[0], d[2], row8n)], axis=0)
        left = jnp.concatenate([z[1], ends(d[1], d[3], row8n)], axis=0)
        for g, (x, l) in enumerate(planes):
            after, prior = y[0, g // 2], y[1, g // 2]
            if g % 2:
                after = pltpu.roll(after, W, 0)
            else:
                prior = pltpu.roll(prior, W, 0)
            x[l, ROWS:XR, 0:COLS] = ends(after, prior, row8)
            at = g * W
            x[l, :, COLS:XC] = sides(
                pltpu.roll(right, 128 - at, 1) if g else right, pltpu.roll(left, 64 - W - at, 1), lane24
            )

    arrive(a_copies, [DOWN])
    begin(a_copies, (1,))

    low_row = iota((LOW, 128), 0).astype(F32)
    high_row = iota((HIGH, 128), 0).astype(F32)

    def hot_columns(at_low):
        return jnp.where(low_row == at_low, 1.0, 0.0).astype(BF16)

    def spread(value, at_high):
        a, b = split2(value)
        there = high_row == at_high
        return jnp.concatenate([jnp.where(there, a, 0.0), jnp.where(there, b, 0.0)], axis=0).astype(BF16)

    def total(x):
        return x[0:HIGH] + x[HIGH:2 * HIGH]

    def scatter(steps, group, blocks_of, row_of, build):
        def step(t, acc):
            blocks = blocks_of(t)
            for first in blocks:
                parts, hots = [], []
                for j in range(group):
                    value, at_high, at_low = row_of(first + j)
                    parts.append(spread(value, at_high))
                    if build:
                        hots.append(hot_columns(at_low))
                lane = pl.ds(pl.multiple_of(first * 128, 128), group * 128)
                if build:
                    columns = jnp.concatenate(hots, axis=1)
                    hot[:, lane] = columns
                else:
                    columns = hot[:, lane]
                acc = acc + dot(jnp.concatenate(parts, axis=1), columns, NT)
            return acc

        sums = total(lax.fori_loop(0, steps, step, jnp.zeros((2 * HIGH, LOW), F32)))
        return jnp.concatenate([sums[0:ROWS], sums[ROWS:HIGH]], axis=1)

    def sheet_parts(x):
        x = jnp.concatenate([x[:, 0:LOW], x[:, LOW:COLS]], axis=0)
        return jnp.concatenate(split2(x), axis=0).astype(BF16)

    def gather(sheet, first, group, high_at, put):
        lane = pl.ds(pl.multiple_of(first * 128, 128), group * 128)
        got = total(dot(sheet, hot[:, lane], NN))
        for j in range(group):
            here = jnp.where(high_row == high_at(first + j), got[:, j * 128:(j + 1) * 128], 0.0)
            put(first + j, jnp.sum(here, axis=0, keepdims=True))

    pair = math.gcd(2, lines)
    group_p = math.gcd(8, nb)

    @pl.when(jnp.logical_not(solid))
    def _():
        def columns(i, _):
            hot[:, pl.ds(pl.multiple_of(i * 128, 128), 128)] = hot_columns(cell_low[pl.ds(i, 1), :])
            return 0

        lax.fori_loop(0, nb, columns, 0, unroll=4)

    @pl.when(jnp.logical_not(solid))
    def _():
        pl.semaphore_wait(ready, wide)

        def send(i, _):
            to = far_first(lax.div(i, wide)) * wide + lax.rem(i, wide)
            pltpu.make_async_remote_copy(
                src_ref=meta_send.at[to], dst_ref=meta_recv.at[my_row],
                send_sem=meta_ssem, recv_sem=meta_rsem.at[my_line], device_id=(last, to, slab), device_id_type=MESH,
            ).start()
            return 0

        lax.fori_loop(0, nb, send, 0)

    arrive(a_copies, [step for step in STEPS if step != DOWN])
    leave(a_copies)
    unpack([(x, l) for l in range(LAYERS) for x in (ua, rx, cx)], yst, zst, dst8)

    def sweep(x, y, source):
        for l in range(LAYERS):
            u = x[l]
            left = pltpu.roll(u, 1, 1)
            around = pltpu.roll(u, 1, 0) + pltpu.roll(u, XR - 1, 0) + left + pltpu.roll(u, XC - 1, 1)
            if l > 0:
                around = around + x[l - 1]
            if l < LAYERS - 1:
                around = around + x[l + 1]
            new = u + rx[l] * (around - 6.0 * u) - cx[l] * (u - left)
            if source and l == 0:
                new = new + (sx[0] - gx[0] * u)
            y[l] = new

    def phase(source):
        for repeat in range(SWEEPS // 2):
            sweep(ua, ub, source)
            sweep(ub, ua, source)

    phase(False)

    @pl.when(jnp.logical_not(solid))
    def _():
        sheet = sheet_parts(ua[0, 0:ROWS, 0:COLS])

        def put(i, row):
            q_send[i] = row * link_p[pl.ds(i, 1), :]

        def step(t, _):
            firsts = [far_first(t * pair + a) * wide for a in range(pair)]
            for first in firsts:
                gather(sheet, first, wide, lambda i: cell_high[pl.ds(i, 1), :], put)
            for first in firsts:
                for j in range(wide):
                    pltpu.make_async_remote_copy(
                        src_ref=q_send.at[first + j], dst_ref=q_recv.at[my_row],
                        send_sem=q_ssem, recv_sem=q_rsem.at[my_line],
                        device_id=(last, first + j, slab), device_id_type=MESH,
                    ).start()
            return 0

        lax.fori_loop(0, lines // pair, step, 0)

    pack([plane(ua, l) for l in range(LAYERS)], uys, uzs)
    begin(u_copies)

    @pl.when(jnp.logical_not(solid))
    def _():
        def packet_row(i):
            one = pl.ds(i, 1)
            return link_p[one, :], cell_high[one, :], cell_low[one, :]

        hsum[...] = scatter(nb // group_p, group_p, lambda t: [t * group_p], packet_row, False)

    def whole(ref, ssem, rsem):
        return pltpu.make_async_remote_copy(
            src_ref=ref, dst_ref=ref, send_sem=ssem, recv_sem=rsem,
            device_id=neighbour(STEPS[0]), device_id_type=MESH,
        )

    def line_in(t, ref, ssem, rsem):
        line = far_first(lines - 1 - t)
        whole(ref.at[pl.ds(line * deep, deep)], ssem, rsem.at[line]).wait_recv()
        return [line * deep]

    def target_row(i, value):
        code = meta_recv[i, 1:2, :]
        high = jnp.floor(code * (1.0 / LOW))
        return value, high, code - float(LOW) * high

    @pl.when(solid)
    def _():
        for copy in slots:
            copy.wait()
        gx[0, 0:ROWS, 0:COLS] = scatter(
            lines, deep, lambda t: line_in(t, meta_recv, meta_ssem, meta_rsem),
            lambda i: target_row(i, meta_recv[i, 0:1, :]), True,
        )
        begin(g_copies)

    @pl.when(solid)
    def _():
        sx[0, 0:ROWS, 0:COLS] = scatter(
            lines, deep, lambda t: line_in(t, q_recv, q_ssem, q_rsem), lambda i: target_row(i, q_recv[i]), False
        )
        begin(s_copies)
        finish(u_copies)
        unpack([(ua, l) for l in range(LAYERS)], uy, uz, udg)
        finish(g_copies)
        unpack_sheet(gx, gy, gz, gdg)
        g = gx[0]
        inverse = 1.0 / (1.0 + g)
        gx[0] = g * inverse
        finish(s_copies)
        unpack_sheet(sx, sy, sz, sdg)
        sx[0] = sx[0] * inverse
        phase(True)
        for l in range(LAYERS):
            out[l] = plane(ua, l)
        sheet = sheet_parts(ua[0, 0:ROWS, 0:COLS])

        def put(i, row):
            ans_send[i] = row

        def step(t, _):
            to_lines = [far_first(t * pair + a) for a in range(pair)]
            for line in to_lines:
                gather(sheet, line * deep, deep, lambda i: target_row(i, None)[1], put)
            for line in to_lines:
                for j in range(deep):
                    pltpu.make_async_remote_copy(
                        src_ref=ans_send.at[line * deep + j], dst_ref=wall_recv.at[brick],
                        send_sem=ans_ssem, recv_sem=ans_rsem.at[my_line],
                        device_id=(j // wide, line * wide + j % wide, slab), device_id_type=MESH,
                    ).start()
            return 0

        lax.fori_loop(0, lines // pair, step, 0)
        whole(ans_send, ans_ssem, ans_rsem.at[0]).wait_send()

    @pl.when(jnp.logical_not(solid))
    def _():
        finish(u_copies)
        unpack([(ua, l) for l in range(LAYERS)], uy, uz, udg)
        phase(False)
        for l in range(1, LAYERS):
            out[l] = plane(ua, l)
        whole(meta_send, meta_ssem, meta_rsem.at[0]).wait_send()
        whole(q_send, q_ssem, q_rsem.at[0]).wait_send()

        def packet_row(i):
            one = pl.ds(i, 1)
            return link_p[one, :] * wall_recv[i], cell_high[one, :], None

        def lines_in(t):
            firsts = []
            for a in range(pair):
                line = far_first(lines - 1 - t * pair - a)
                ref = wall_recv.at[pl.ds(line * wide, wide)]
                whole(ref, ans_ssem, ans_rsem.at[line]).wait_recv()
                firsts.append(line * wide)
            return firsts

        q = scatter(lines // pair, wide, lines_in, packet_row, False)
        h = hsum[...]
        u = ua[0, 0:ROWS, 0:COLS]
        out[0] = u + (q - h * u) / (1.0 + h)


def body(nd, nb, ns, heat, ratio, courant, voxel, owner, target, link, tally):
    groups = voxel.size // 128
    slots = [x.reshape(groups, 128) for x in (voxel, owner, target, link)]
    rows_in = (nd - 1) * nb
    most = max(rows_in, nb)
    lines = nb // math.gcd(4, nb)
    vm = pltpu.VMEM
    sem = pltpu.SemaphoreType.DMA

    def landings(planes):
        return [vm((2, planes // 2, 8, COLS), F32), vm((2, ROWS, 128), F32), vm((4, 8, 128), F32)]

    def packing(planes):
        return [vm((2, planes // 2, 8, COLS), F32), vm((ROWS, 128), F32)]

    sheet = [vm((2, 1, 8, COLS), F32), vm((2, 1, ROWS, 128), F32), vm((4, 1, 8, 128), F32)]

    field = vm((LAYERS, XR, XC), F32)
    scratch = (
        [field] * 4 + [vm((1, XR, XC), F32)] * 2
        + [vm((groups, 128), I32)] * 3 + [vm((groups, 128), F32), vm((1, 1, 1), I32)]
        + packing(3 * LAYERS) + landings(3 * LAYERS) + packing(LAYERS) + landings(LAYERS) + sheet * 2
        + [vm((LOW, most * CAP), BF16), vm((groups * nb, 128), F32), vm((groups * nb, 256), F32)]
        + [vm((PARTS * nb, groups * 128), BF16), vm((128, groups * 128), BF16)]
        + [vm((nb, CAP), F32)] * 3 + [vm((ROWS, COLS), F32)]
        + [vm((nb, 2, CAP), F32), vm((nb, 1, CAP), F32), vm((rows_in, 2, CAP), F32), vm((rows_in, 1, CAP), F32)]
        + [vm((rows_in, 1, CAP), F32), vm((nb, 1, CAP), F32)]
        + [sem((3,)), sem((5,))]
        + [sem((8,))] * 8
        + [pltpu.SemaphoreType.REGULAR] + [sem, sem((lines,))] * 3
    )
    hbm = pl.BlockSpec(memory_space=pl.ANY)
    return pl.pallas_call(
        functools.partial(kernel, nd, nb, ns),
        out_shape=pltpu.VMEM(heat.shape, F32),
        in_specs=[hbm] * 8,
        out_specs=pl.BlockSpec(memory_space=pltpu.VMEM),
        scratch_shapes=scratch,
        compiler_params=pltpu.CompilerParams(
            collective_id=0, has_side_effects=True, vmem_limit_bytes=VMEM_BYTES
        ),
    )(heat, ratio, courant, *slots, tally)


def solution(mesh):
    nd, nb, ns = (mesh.shape[a] for a in ("dom", "brick", "slab"))
    where = P("dom", "brick", "slab")
    return jax.shard_map(
        functools.partial(body, nd, nb, ns),
        mesh=mesh,
        in_specs=(where,) * 8,
        out_specs=where,
        check_vma=False,
    )
```
